32 devices in a mesh: slide: 2 (over x), space: 8 (over z, y), tensor: 2 (over core).
Axes of the slice: x: 2, y: 2, z: 4, core: 2. Of those that a mesh axis runs over, the one named last changes fastest.
Arguments:
- features: bfloat16 [64, 16, 16, 768], P(('slide', 'space'), None, None, 'tensor'), parts along dimension 0, may hold values from -6 to 6
- dw_kernel: float32 [49, 768], P(None, 'tensor'), may hold values from -0.875 to 0.875
- dw_bias: float32 [768], P('tensor'), may hold values from -3 to 3
- ln_gain: float32 [768], replicated, may hold values from 0.5 to 1.5
- ln_bias: float32 [768], replicated, may hold values from -2 to 2
- w_up: bfloat16 [768, 3072], P(None, 'tensor'), may hold values from -0.21875 to 0.21875
- up_bias: float32 [3072], P('tensor'), may hold values from -3 to 3
- w_down: bfloat16 [768, 3072], P(None, 'tensor'), may hold values from -0.109375 to 0.109375
- down_bias: float32 [768], P('tensor'), may hold values from -2 to 2
- layer_scale: float32 [768], P('tensor'), may hold values from 0.3 to 1.5
- cotangent: bfloat16 [64, 16, 16, 768], P(('slide', 'space'), None, None, 'tensor'), parts along dimension 0, may hold values from -4 to 4
- neighbors: int32 [64, 8], P('slide'), parts along dimension 0, may hold values from -1 to 31, as said below
- tissue_count: int32 [16], P('slide'), parts along dimension 0, may hold values from 1 to 4, as said below
Outputs:
- block_out: bfloat16 [64, 16, 16, 768], P(('slide', 'space'), None, None, 'tensor'), parts along dimension 0
- grad_features: bfloat16 [64, 16, 16, 768], P(('slide', 'space'), None, None, 'tensor'), parts along dimension 0
- grad_up: float32 [1536, 3072], P(('slide', 'space'), 'tensor'), parts along dimension 0
- grad_down: float32 [1536, 3072], P(('slide', 'space'), 'tensor'), parts along dimension 0
- grad_kernel: float32 [98, 768], P('slide', 'tensor'), parts along dimension 0
The draws below stay inside these ranges and needn't reach their ends.
There are 2 independent parts, one for each index of `slide`. The reference program is written for one: setup_inputs(seed, part) draws one part's arguments, and reference() takes and returns one part's arrays. A program takes and returns all parts, laid end to end along the dimension named above; an argument that names none is the same for every part. Nothing has to cross between parts.
Inputs may be any that keep to these rules, and one draw needn't show every extreme that they name: `neighbors`: the tiles lie on a grid of 2 by 2 blocks with R block rows and 8 / R block columns, R the largest divisor of 8 not above its square root; device d of space holds the block at block row d // (8 / R) and block column d mod (8 / R), its slot 2 r + q (slot s belongs to device s // 4) at row r and column q of the block. Entry [s, k] is the slot of the tissue tile beside slot s's tile on this grid in direction k (0 north, 1 south, 2 west, 3 east, 4 north-west, 5 north-east, 6 south-west, 7 south-east), or -1 where that place lies outside the grid or holds no tissue; empty slots have no neighbours. The tissue tiles of device d fill its first tissue_count[d] slots; its other slots are empty.
All inputs are finite; a program needn't handle non-finite values.
Results may differ from the reference program's by a relative error of at most 0.008.
Values may be sent and summed in bfloat16 or wider, within the bound.
No kernel may reach another device: no remote copies, remote signals or barrier semaphores. Data moves between devices by JAX's collectives and lax.ppermute only.
A program may use at most 128 MiB of HBM per device.

```python
import math
import jax
import jax.numpy as jnp
from jax import lax

CHANNELS = 768
MLP_WIDTH = 3072
KERNEL = 7
TILE_SIDE = 16
TILES_DEV = 4
TAPS = 49
TILES = 32
N_SPACE = 8


DIRECTIONS = ((-1, 0), (1, 0), (0, -1), (0, 1), (-1, -1), (-1, 1), (1, -1), (1, 1))


def tile_layout(key):
    block_rows = max((divisor for divisor in range(1, math.isqrt(N_SPACE) + 1) if N_SPACE % divisor == 0))
    block_cols = N_SPACE // block_rows
    counts = jax.random.randint(jax.random.fold_in(key, 12), (N_SPACE,), 1, TILES_DEV + 1).astype(jnp.int32)
    full_pick = jax.random.permutation(jax.random.fold_in(key, 11), N_SPACE).astype(jnp.int32)
    counts = counts.at[full_pick[0]].set(TILES_DEV).at[full_pick[1]].set(TILES_DEV)
    slot_ids = jnp.arange(TILES, dtype=jnp.int32)
    device = slot_ids // TILES_DEV
    local_slot = slot_ids % TILES_DEV
    grid_row = device // block_cols * 2 + local_slot // 2
    grid_col = device % block_cols * 2 + local_slot % 2
    present = local_slot < counts[device]
    columns = []
    for direction in range(8):
        step_row, step_col = DIRECTIONS[direction]
        other_row = grid_row + step_row
        other_col = grid_col + step_col
        inside = (other_row >= 0) & (other_row < 2 * block_rows) & (other_col >= 0) & (other_col < 2 * block_cols)
        clip_row = jnp.clip(other_row, 0, 2 * block_rows - 1)
        clip_col = jnp.clip(other_col, 0, 2 * block_cols - 1)
        other_dev = clip_row // 2 * block_cols + clip_col // 2
        other_local = clip_row % 2 * 2 + clip_col % 2
        other_here = other_local < counts[other_dev]
        columns.append(jnp.where(inside & present & other_here, other_dev * TILES_DEV + other_local, -1))
    return (counts, jnp.stack(columns, axis=1).astype(jnp.int32))


def draw_neighbors(key, part):
    return tile_layout(key)[1]


def draw_tissue_count(key, part):
    return tile_layout(key)[0]


def with_spikes(result, stream_key, source, target, parts, factor):
    owner, partner = [(jnp.arange(result.shape[axis_at]) // (result.shape[axis_at] // parts)).reshape([-1 if axis == axis_at else 1 for axis in range(result.ndim)]) for axis_at in (source, target)]
    chosen = jax.random.permutation(stream_key, parts)[partner]
    strong = (owner == chosen) | (owner == (partner + parts // 2) % parts)
    return jnp.where(strong, factor * result, result)


def steps_of(key, extent, cuts, low, high):
    def one(axis_at, parts):
        draws = jax.random.uniform(jax.random.fold_in(jax.random.fold_in(key, 6), axis_at), (parts,), jnp.float32, low / len(cuts), high / len(cuts))
        return jnp.repeat(jnp.exp(draws), extent[axis_at] // parts).reshape((-1,) + (1,) * (len(extent) - axis_at - 1))

    loudness = one(*cuts[0])
    for cut in cuts[1:]:
        loudness = loudness * one(*cut)
    return loudness


def centred(own_key, extent, deviation, bound, cuts=(), kind=jnp.bfloat16):
    loudness = steps_of(own_key, extent, cuts, -0.22, 0.18) if cuts else 1.0
    drawn = jax.random.normal(own_key, extent, jnp.float32) * deviation * loudness
    return jnp.minimum(jnp.maximum(drawn, -bound), bound).astype(kind)


def heavy_noise(stream_key, extent, spread, most, shards, heavy, kind=jnp.bfloat16):
    values = spread * jax.random.normal(stream_key, extent, jnp.float32)
    if shards:
        values = values * steps_of(stream_key, extent, shards, -0.22, 0.18)
    return jnp.clip(with_spikes(values, jax.random.fold_in(stream_key, 3), *heavy), -most, most).astype(kind)


def setup_inputs(seed: int = 0, part: int = 0) -> dict:
    streams_of = jax.random.split(jax.random.key(seed), 14)
    own_keys = jax.random.split(jax.random.fold_in(streams_of[13], part), 14)
    features = centred(own_keys[0], (TILES, TILE_SIDE, TILE_SIDE, CHANNELS), 1.0, 6.0, ((0, 8), (3, 2)))
    dw_kernel = centred(streams_of[1], (TAPS, CHANNELS), TAPS ** -0.5, 0.875, ((1, 2),), jnp.float32)
    dw_bias = centred(streams_of[2], (CHANNELS,), 0.5, 3.0, ((0, 2),), jnp.float32)
    ln_gain = jnp.clip(1.0 + 0.1 * jax.random.normal(streams_of[3], (CHANNELS,), jnp.float32), 0.5, 1.5)
    ln_bias = centred(streams_of[4], (CHANNELS,), 0.3, 2.0, (), jnp.float32)
    w_up = centred(streams_of[5], (CHANNELS, MLP_WIDTH), CHANNELS ** -0.5, 0.21875, ((1, 2),))
    up_bias = centred(streams_of[6], (MLP_WIDTH,), 0.5, 3.0, ((0, 2),), jnp.float32)
    w_down = centred(streams_of[7], (CHANNELS, MLP_WIDTH), MLP_WIDTH ** -0.5, 0.109375, ((1, 2),))
    down_bias = centred(streams_of[8], (CHANNELS,), 0.3, 2.0, ((0, 2),), jnp.float32)
    layer_scale = jnp.clip(jnp.exp(math.log(1.5) - 1.60943787 * jax.random.uniform(streams_of[9], (CHANNELS,), jnp.float32) ** steps_of(streams_of[9], (CHANNELS,), ((0, 2),), -0.2, 0.2)), 0.3, 1.5)
    cotangent = heavy_noise(own_keys[10], (TILES, TILE_SIDE, TILE_SIDE, CHANNELS), 0.5, 4.0, ((0, 8), (3, 2)), (0, 3, 8, 2.0))
    neighbors = draw_neighbors(jax.random.fold_in(jax.random.fold_in(streams_of[13], part), 71), part)
    tissue_count = draw_tissue_count(jax.random.fold_in(jax.random.fold_in(streams_of[13], part), 71), part)
    return dict(features=features, dw_kernel=dw_kernel, dw_bias=dw_bias, ln_gain=ln_gain, ln_bias=ln_bias, w_up=w_up, up_bias=up_bias, w_down=w_down, down_bias=down_bias, layer_scale=layer_scale, cotangent=cotangent, neighbors=neighbors, tissue_count=tissue_count)


DIRECTIONS = ((-1, 0), (1, 0), (0, -1), (0, 1), (-1, -1), (-1, 1), (1, -1), (1, 1))
root_half = 0.7071067811865476
density_norm = 0.3989422804014327

def rim_range(side_len, facing, rim_width):
    if facing < 0:
        return (0, rim_width)
    if facing > 0:
        return (side_len - rim_width, side_len)
    return (0, side_len)

def cut_rim(blocks, direction, facing_sign, rim_width):
    step_row, step_col = DIRECTIONS[direction]
    row_lo, row_hi = rim_range(blocks.shape[1], facing_sign * step_row, rim_width)
    col_lo, col_hi = rim_range(blocks.shape[2], facing_sign * step_col, rim_width)
    return blocks[:, row_lo:row_hi, col_lo:col_hi, :]

def assemble(center, rim_parts):
    top_band = jnp.concatenate([rim_parts[4], rim_parts[0], rim_parts[5]], axis=2)
    mid_band = jnp.concatenate([rim_parts[2], center, rim_parts[3]], axis=2)
    bottom_band = jnp.concatenate([rim_parts[6], rim_parts[1], rim_parts[7]], axis=2)
    return jnp.concatenate([top_band, mid_band, bottom_band], axis=1)

def depthwise(padded, kernel, side_len, flipped):
    rim_width = KERNEL // 2
    running = jnp.zeros((padded.shape[0], side_len, side_len, padded.shape[3]), jnp.float32)
    for row_tap in range(KERNEL):
        for col_tap in range(KERNEL):
            row_at = 2 * rim_width - row_tap if flipped else row_tap
            col_at = 2 * rim_width - col_tap if flipped else col_tap
            window = padded[:, row_at:row_at + side_len, col_at:col_at + side_len, :].astype(jnp.float32)
            running = running + window * kernel[row_tap * KERNEL + col_tap]
    return running

def kernel_terms(padded, conv_grad, side_len):
    grad_values = conv_grad.astype(jnp.float32)
    rows_out = []
    for row_tap in range(KERNEL):
        for col_tap in range(KERNEL):
            window = padded[:, row_tap:row_tap + side_len, col_tap:col_tap + side_len, :].astype(jnp.float32)
            rows_out.append(lax.optimization_barrier(jnp.sum(window * grad_values, axis=(0, 1, 2))))
    return jnp.stack(rows_out, axis=0)

def gelu_slope(values):
    cumulative = 0.5 * (1.0 + lax.erf(values * root_half))
    density = jnp.exp(-0.5 * values * values) * density_norm
    return cumulative + values * density

def reference(features, dw_kernel, dw_bias, ln_gain, ln_bias, w_up, up_bias, w_down, down_bias, layer_scale, cotangent, neighbors, tissue_count):
    rim_width = KERNEL // 2
    slot_ids = jnp.arange(TILES, dtype=jnp.int32)
    present = (slot_ids % TILES_DEV < tissue_count[slot_ids // TILES_DEV]).astype(jnp.float32)
    row_ok = jnp.repeat(present, TILE_SIDE * TILE_SIDE)[:, None]

    def surround(blocks):
        rim_parts = []
        for direction in range(8):
            source = neighbors[:, direction]
            rim_piece = jnp.take(cut_rim(blocks, direction, -1, rim_width), jnp.maximum(source, 0), axis=0)
            rim_parts.append(jnp.where((source >= 0)[:, None, None, None], rim_piece, jnp.zeros((), blocks.dtype)))
        return assemble(blocks, rim_parts)
    feature_pad = surround(features)
    conv_out = (depthwise(feature_pad, dw_kernel, TILE_SIDE, False) + dw_bias).astype(jnp.bfloat16)
    conv_rows = conv_out.reshape(-1, CHANNELS).astype(jnp.float32)
    row_mean = lax.optimization_barrier(jnp.mean(conv_rows, axis=1, keepdims=True))
    centered = conv_rows - row_mean
    row_var = lax.optimization_barrier(jnp.mean(centered * centered, axis=1, keepdims=True))
    inverse_std = lax.rsqrt(row_var + 1e-06)
    normalized = centered * inverse_std
    normed = (normalized * ln_gain + ln_bias).astype(jnp.bfloat16)
    hidden = jnp.dot(normed, w_up, preferred_element_type=jnp.float32) + up_bias
    active = jax.nn.gelu(hidden, approximate=False).astype(jnp.bfloat16)
    branch = lax.dot_general(active, w_down, (((1,), (1,)), ((), ())), preferred_element_type=jnp.float32) + down_bias
    residual = features.reshape(-1, CHANNELS).astype(jnp.float32)
    block_out = ((residual + layer_scale * branch) * row_ok).astype(jnp.bfloat16).reshape(features.shape)
    grad_out = cotangent.reshape(-1, CHANNELS).astype(jnp.float32) * row_ok
    branch_grad = (grad_out * layer_scale).astype(jnp.bfloat16)
    grad_scale = lax.rsqrt(jnp.float32(TILE_SIDE * TILE_SIDE) * jnp.sum(tissue_count).astype(jnp.float32))
    grad_down = lax.dot_general(branch_grad, active, (((0,), (0,)), ((), ())), preferred_element_type=jnp.float32) * grad_scale
    act_grad = jnp.dot(branch_grad, w_down, preferred_element_type=jnp.float32)
    pre_grad = (act_grad * gelu_slope(hidden)).astype(jnp.bfloat16)
    grad_up = lax.dot_general(normed, pre_grad, (((0,), (0,)), ((), ())), preferred_element_type=jnp.float32) * grad_scale
    norm_grad = lax.dot_general(pre_grad, w_up, (((1,), (1,)), ((), ())), preferred_element_type=jnp.float32)
    scaled = norm_grad * ln_gain
    conv_grad = inverse_std * (scaled - lax.optimization_barrier(jnp.mean(scaled, axis=1, keepdims=True)) - normalized * lax.optimization_barrier(jnp.mean(scaled * normalized, axis=1, keepdims=True)))
    conv_grad = conv_grad.astype(jnp.bfloat16).reshape(features.shape)
    grad_pad = surround(conv_grad)
    back_conv = depthwise(grad_pad, dw_kernel, TILE_SIDE, True)
    grad_features = ((grad_out.reshape(features.shape) + back_conv) * present[:, None, None, None]).astype(jnp.bfloat16)
    grad_kernel = kernel_terms(feature_pad, conv_grad, TILE_SIDE) * grad_scale
    return (block_out, grad_features, grad_up, grad_down, grad_kernel)
```

```python
import functools
import math

import jax
import jax.numpy as jnp
from jax import lax
from jax.experimental import pallas as pl
from jax.experimental.pallas import tpu as pltpu
from jax.sharding import PartitionSpec as P

KERNEL = 7
RIM = 3
LANES = 128
F32 = jnp.float32
BF16 = jnp.bfloat16
VMEM_BYTES = 60 * 1024 * 1024

TAIL_P = 0.39
TAIL = (
    0.2353252521737435,
    0.0913882086982987,
    0.6495599070595628,
    -0.635400901941762,
    0.8866647490628095,
    -0.2275372167464003,
)
ROOT_HALF = 0.7071067811865476
DENSITY = 0.3989422804014327


def smem():
    return pl.BlockSpec(memory_space=pltpu.SMEM)


def whole(shape):
    return pl.BlockSpec(shape, lambda *_: (0,) * len(shape))


def call(body, grid, ins, outs, shapes, scratch, flops, nbytes, args):
    return pl.pallas_call(
        body,
        grid=grid,
        in_specs=ins,
        out_specs=outs,
        out_shape=shapes,
        scratch_shapes=scratch,
        compiler_params=pltpu.CompilerParams(vmem_limit_bytes=VMEM_BYTES),
        cost_estimate=pl.CostEstimate(flops=flops, bytes_accessed=nbytes, transcendentals=0),
    )(*args)


def phi_pair(h):
    e = jnp.exp(h * h * -0.5)
    den = 1.0 + (TAIL_P * ROOT_HALF) * jnp.abs(h)
    t = pl.reciprocal(den, approx=True)
    t = t * (2.0 - den * t)
    acc = jnp.full_like(h, 0.5 * TAIL[5])
    for coef in TAIL[4::-1]:
        acc = acc * t + 0.5 * coef
    tail = acc * t * e
    return jnp.where(h >= 0, 1.0 - tail, tail), e


def store_rims(odd_row, top, bottom, near_ref, far_ref):
    @pl.when(odd_row == 0)
    def _():
        for side in range(2):
            near_ref[:, side * 16 : side * 16 + 16, :] = bottom[side]
            far_ref[:, side * 16 : side * 16 + 16, :] = top[side]

    @pl.when(odd_row == 1)
    def _():
        for side in range(2):
            near_ref[:, side * 16 : side * 16 + 16, :] = top[side]
            far_ref[:, side * 16 : side * 16 + 16, :] = bottom[side]


def prep_body(info, x_ref, cot_ref, scale_ref, near_ref, far_ref, bg_ref):
    count = info[3]

    def masked(slot, lo, hi):
        return (x_ref[slot, lo:hi].astype(F32) * (slot < count).astype(F32)).astype(BF16)

    store_rims(
        info[1],
        [masked(0, 0, 3), masked(1, 0, 3)],
        [masked(2, 13, 16), masked(3, 13, 16)],
        near_ref,
        far_ref,
    )
    for slot in range(4):
        rows = slice(slot * 256, slot * 256 + 256)
        ok = (slot < count).astype(F32)
        bg_ref[rows, :] = (cot_ref[rows, :].astype(F32) * (ok * scale_ref[...])).astype(BF16)


def side_body(masked, info, x_ref, near_ref, far_ref, a_ref, b_ref, east, west, packed):
    count = info[3]
    odd_row = info[1]
    for slot in range(4):
        value = x_ref[slot].astype(F32)
        if masked:
            value = value * (slot < count).astype(F32)
        rows = slice(RIM + (slot // 2) * 16, RIM + (slot // 2) * 16 + 16)
        if slot % 2:
            east[rows] = value[:, 8:16, :]
        else:
            west[rows] = value[:, 0:8, :]
    near = near_ref[...].astype(F32)
    far = far_ref[...].astype(F32)
    is_odd = (odd_row == 1).astype(F32)
    north = near * is_odd + far * (1.0 - is_odd)
    south = near * (1.0 - is_odd) + far * is_odd
    east[0:3] = north[:, 24:32, :]
    west[0:3] = north[:, 0:8, :]
    east[35:38] = south[:, 24:32, :]
    west[35:38] = south[:, 0:8, :]
    zero = jnp.zeros_like(east[38:40])
    east[38:40] = zero
    west[38:40] = zero

    def pack(out_ref, source, at):
        packed[:, 0:4, :] = source[0:20, at : at + 4, :]
        packed[:, 4:8, :] = source[20:40, at : at + 4, :]
        out_ref[...] = packed[...].reshape(out_ref.shape).astype(BF16)

    @pl.when(info[2] == 0)
    def _():
        pack(a_ref, east, 4)
        pack(b_ref, west, 0)

    @pl.when(info[2] == 1)
    def _():
        pack(a_ref, west, 0)
        pack(b_ref, east, 4)


def conv_body(backward, info, x_ref, near_ref, far_ref, a_ref, b_ref, w_ref, last_ref, out_ref, left_ref, image, weights):
    count = info[3]
    for slot in range(4):
        value = x_ref[slot].astype(F32)
        if not backward:
            value = value * (slot < count).astype(F32)
        r, q = slot // 2, slot % 2
        image[RIM + 16 * r : RIM + 16 * r + 16, 8 + 16 * q : 24 + 16 * q, :] = value
    near = near_ref[...].astype(F32)
    far = far_ref[...].astype(F32)
    is_odd = (info[1] == 1).astype(F32)
    image[0:3, 8:40, :] = near * is_odd + far * (1.0 - is_odd)
    image[35:38, 8:40, :] = near * (1.0 - is_odd) + far * is_odd
    first = a_ref[...].astype(F32).reshape(20, 8, LANES)
    second = b_ref[...].astype(F32).reshape(20, 8, LANES)
    odd_col = (info[2] == 1).astype(F32)
    from_left = first * odd_col + second * (1.0 - odd_col)
    from_right = first * (1.0 - odd_col) + second * odd_col
    image[20:40, 0:8, :] = from_left
    image[0:20, 4:8, :] = from_left[:, 0:4, :]
    image[0:20, 40:48, :] = from_right
    image[20:40, 40:44, :] = from_right[:, 4:8, :]

    for b in range(KERNEL):
        value = image[0:38, 5 + b : 37 + b, :].astype(BF16).reshape(19, 2, 32, LANES)
        for par in range(2):
            at = b * 256 + par * LANES
            left_ref[0, :, at : at + LANES] = value[:, par].reshape(608, LANES)

    eye = lax.broadcasted_iota(jnp.int32, (LANES, LANES), 0) == lax.broadcasted_iota(
        jnp.int32, (LANES, LANES), 1
    )
    empty = jnp.zeros((LANES, LANES), BF16)
    for a in range(-1, KERNEL + 1):
        for b in range(KERNEL):
            if 0 <= a < KERNEL:
                tap = (KERNEL - 1 - a) * KERNEL + KERNEL - 1 - b if backward else a * KERNEL + b
                block = jnp.where(eye, w_ref[tap : tap + 1, :], 0.0).astype(BF16)
            else:
                block = empty
            for o in range(2):
                r = a + o
                if 0 <= r < 8:
                    at = (r // 2) * 1792 + b * 256 + (r % 2) * LANES
                    weights[at : at + LANES, o * LANES : (o + 1) * LANES] = block
    acc = None
    for q in range(4):
        term = jnp.dot(
            left_ref[0, 32 * q : 32 * q + 512, :],
            weights[1792 * q : 1792 * (q + 1), :],
            preferred_element_type=F32,
        )
        acc = term if acc is None else acc + term
    acc = acc.reshape(16, 32, 256)
    for slot in range(4):
        r, q = slot // 2, slot % 2
        for o in range(2):
            value = acc[8 * r : 8 * r + 8, 16 * q : 16 * q + 16, o * LANES : (o + 1) * LANES]
            if backward:
                value = (value + last_ref[slot, :, o].astype(F32)) * (slot < count).astype(F32)
            else:
                value = value + last_ref[...].reshape(1, 1, LANES)
            out_ref[slot, :, o] = value.astype(BF16)


def taps_body(g_ref, left_ref, out_ref, paired):
    for slot in range(4):
        r, q = slot // 2, slot % 2
        for o in range(2):
            paired[8 * r : 8 * r + 8, 16 * q : 16 * q + 16, o * LANES : (o + 1) * LANES] = g_ref[slot, :, o].astype(F32)
    turned = paired[...].reshape(512, 256).T.astype(BF16)
    eye = lax.broadcasted_iota(jnp.int32, (LANES, LANES), 0) == lax.broadcasted_iota(
        jnp.int32, (LANES, LANES), 1
    )
    sums = {}
    for q in range(4):
        prod = jnp.dot(turned, left_ref[0, 32 * q : 32 * q + 512, :], preferred_element_type=F32)
        for b in range(KERNEL):
            for par in range(2):
                for o in range(2):
                    a = 2 * q + par - o
                    if 0 <= a < KERNEL:
                        block = prod[o * LANES : (o + 1) * LANES, b * 256 + par * LANES : b * 256 + (par + 1) * LANES]
                        row = jnp.sum(jnp.where(eye, block, 0.0), axis=0, keepdims=True)
                        key = a * KERNEL + b
                        if key in sums:
                            out_ref[key : key + 1, :] = sums.pop(key) + row
                        else:
                            sums[key] = row
    out_ref[49:56, :] = jnp.zeros((7, LANES), F32)


def pick(second, own, other):
    s = second.astype(F32)
    own = own.astype(F32)
    other = other.astype(F32)
    low = own * (1.0 - s) + other * s
    high = own * s + other * (1.0 - s)
    return jnp.concatenate([low, high], axis=1)


def grad_in_body(info, own_ref, other_ref, w_ref, out_ref, turned_ref):
    full = pick(info[0] == 1, own_ref[...], other_ref[...])
    turned_ref[...] = full.T.astype(BF16)
    out_ref[...] = jnp.dot(full.astype(BF16), w_ref[...], preferred_element_type=F32)


def mlp_body(
    info, own_ref, other_ref, gain_ref, shift_ref, up_ref, bias_ref, down_ref, in_ref,
    turned_ref, act_ref, pre_ref, keep_ref, send_ref, sums_ref, bkeep_ref, bsend_ref,
):
    second = info[0] == 1
    rows = pick(second, own_ref[...], other_ref[...])
    mean = jnp.mean(rows, axis=1, keepdims=True)
    centered = rows - mean
    var = jnp.mean(centered * centered, axis=1, keepdims=True)
    normalized = centered * lax.rsqrt(var + 1e-06)
    value = normalized * gain_ref[...] + shift_ref[...]
    turned_ref[...] = value.T.astype(BF16)
    normed = value.astype(BF16)
    units = up_ref.shape[1]
    step = 512
    back = None
    branch = None
    dims = (((1,), (1,)), ((), ()))
    for at in range(0, units, step):
        cols = slice(at, at + step)
        hidden = jnp.dot(normed, up_ref[:, cols], preferred_element_type=F32) + bias_ref[:, cols]
        phi, e = phi_pair(hidden)
        active = (hidden * phi).astype(BF16)
        act_ref[:, cols] = active
        pre = (in_ref[:, cols] * (phi + hidden * (e * DENSITY))).astype(BF16)
        pre_ref[:, cols] = pre
        one = lax.dot_general(pre, up_ref[:, cols], dims, preferred_element_type=F32)
        two = lax.dot_general(active, down_ref[:, cols], dims, preferred_element_type=F32)
        back = one if back is None else back + one
        branch = two if branch is None else branch + two
    scaled = back * gain_ref[...]
    first = jnp.sum(scaled, axis=1, keepdims=True)
    other = jnp.sum(scaled * normalized, axis=1, keepdims=True)
    lane = lax.broadcasted_iota(jnp.int32, sums_ref.shape, 1)
    sums_ref[...] = jnp.where(lane == 0, first, other)
    half = keep_ref.shape[1]
    s = second.astype(F32)

    def split(value):
        low, high = value[:, :half], value[:, half:]
        return low * (1.0 - s) + high * s, low * s + high * (1.0 - s)

    keep, send = split(back)
    keep_ref[...] = keep
    send_ref[...] = send.astype(BF16)
    keep, send = split(branch)
    bkeep_ref[...] = keep
    bsend_ref[...] = send.astype(BF16)


def outer_body(left_ref, right_ref, out_ref):
    out_ref[...] = jnp.dot(left_ref[...], right_ref[...], preferred_element_type=F32).astype(BF16)


def norm_back_body(info, own_ref, other_ref, keep_ref, got_ref, mine_ref, sums_ref, gain_ref, out_ref, near_ref, far_ref):
    own = own_ref[...].astype(F32)
    other = other_ref[...].astype(F32)
    total = 2.0 * own.shape[1]
    mean = (jnp.sum(own, axis=1, keepdims=True) + jnp.sum(other, axis=1, keepdims=True)) / total
    own = own - mean
    other = other - mean
    var = (jnp.sum(own * own, axis=1, keepdims=True) + jnp.sum(other * other, axis=1, keepdims=True)) / total
    inverse = lax.rsqrt(var + 1e-06)
    normalized = own * inverse
    scaled = (keep_ref[...] + got_ref[...].astype(F32)) * gain_ref[...]
    both = (mine_ref[...] + sums_ref[...]) / total
    grad = inverse * (scaled - both[:, 0:1] - normalized * both[:, 1:2])
    out_ref[...] = grad.astype(BF16)
    tile = grad.reshape(16, 16, grad.shape[1])
    odd_row = info[1]
    slot = pl.program_id(0)
    for side in range(2):
        cols = slice(side * 16, side * 16 + 16)

        @pl.when(slot == side)
        def _():
            top = tile[0:3].astype(BF16)

            @pl.when(odd_row == 0)
            def _():
                far_ref[:, cols, :] = top

            @pl.when(odd_row == 1)
            def _():
                near_ref[:, cols, :] = top

        @pl.when(slot == side + 2)
        def _():
            bottom = tile[13:16].astype(BF16)

            @pl.when(odd_row == 0)
            def _():
                near_ref[:, cols, :] = bottom

            @pl.when(odd_row == 1)
            def _():
                far_ref[:, cols, :] = bottom


def on_device(
    features, dw_kernel, dw_bias, ln_gain, ln_bias, w_up, up_bias, w_down, down_bias, layer_scale,
    cotangent, neighbors, tissue_count,
):
    tiles_dev, side, _, chans = features.shape
    units = w_up.shape[1]
    cells = tiles_dev * side * side
    devices = lax.axis_size("space")
    me = lax.axis_index("space")
    tensor_index = lax.axis_index("tensor")
    block_rows = max(d for d in range(1, math.isqrt(devices) + 1) if devices % d == 0)
    block_cols = devices // block_rows
    count = lax.dynamic_index_in_dim(tissue_count, me, 0, keepdims=False)
    info = jnp.stack([tensor_index, (me // block_cols) % 2, (me % block_cols) % 2, count]).astype(jnp.int32)
    blocks = chans // LANES

    def sds(shape, dtype):
        return jax.ShapeDtypeStruct(shape, dtype)

    def across(value):
        return lax.ppermute(value, "tensor", [(0, 1), (1, 0)])

    def paired(value, along_rows, round_at):
        size = block_rows if along_rows else block_cols
        pairs = []
        for d in range(devices):
            place = d // block_cols if along_rows else d % block_cols
            other = place + 1 if place % 2 == round_at else place - 1
            if 0 <= other < size:
                pairs.append((d, d + (other - place) * (block_cols if along_rows else 1)))
        if not pairs:
            return jnp.zeros_like(value)
        return lax.ppermute(value, "space", pairs)

    rim_shape = (RIM, 2 * side, chans)
    pack_shape = (160, chans)

    def sides(x, near, far, masked):
        return call(
            functools.partial(side_body, masked),
            (1,),
            [smem(), whole(features.shape), whole(rim_shape), whole(rim_shape)],
            [whole(pack_shape)] * 2,
            [sds(pack_shape, BF16)] * 2,
            [pltpu.VMEM((40, 8, chans), F32), pltpu.VMEM((40, 8, chans), F32), pltpu.VMEM((20, 8, chans), F32)],
            1000000, 2000000, (info, x, near, far),
        )

    split_shape = (4, 8, 2, side, chans)
    split_spec = pl.BlockSpec((4, 8, 2, side, LANES), lambda c: (0, 0, 0, 0, c))

    def conv(x, near, far, one, two, last, backward):
        if backward:
            last_spec = split_spec
        else:
            last_spec = pl.BlockSpec((1, LANES), lambda c: (0, c))
        rim_spec = pl.BlockSpec((RIM, 2 * side, LANES), lambda c: (0, 0, c))
        pack_spec = pl.BlockSpec((160, LANES), lambda c: (0, c))
        outs = [split_spec]
        shapes = [sds(split_shape, BF16)]
        scratch = [pltpu.VMEM((40, 48, LANES), F32), pltpu.VMEM((4 * 1792, 256), BF16)]
        if backward:
            scratch = [pltpu.VMEM((1, 608, 1792), BF16)] + scratch
        else:
            outs.append(pl.BlockSpec((1, 608, 1792), lambda c: (c, 0, 0)))
            shapes.append(sds((blocks, 608, 1792), BF16))
        return call(
            functools.partial(conv_body, backward),
            (blocks,),
            [
                smem(),
                pl.BlockSpec((4, side, side, LANES), lambda c: (0, 0, 0, c)),
                rim_spec, rim_spec, pack_spec, pack_spec,
                pl.BlockSpec((KERNEL * KERNEL, LANES), lambda c: (0, c)),
                last_spec,
            ],
            outs, shapes, scratch,
            5600000000, 10000000, (info, x, near, far, one, two, dw_kernel, last),
        )

    near_send, far_send, branch_grad = call(
        prep_body,
        (1,),
        [smem(), whole(features.shape), whole((cells, chans)), whole((1, chans))],
        [whole(rim_shape), whole(rim_shape), whole((cells, chans))],
        [sds(rim_shape, BF16), sds(rim_shape, BF16), sds((cells, chans), BF16)],
        [], 1000000, 3000000,
        (info, features, cotangent.reshape(cells, chans), layer_scale.reshape(1, chans)),
    )
    near = paired(near_send, True, 0)
    far = paired(far_send, True, 1)
    other_grad = across(branch_grad)
    one_send, two_send = sides(features, near, far, True)
    one = paired(one_send, False, 0)
    two = paired(two_send, False, 1)

    row_block = pl.BlockSpec((256, chans), lambda i: (i, 0))
    unit_rows = pl.BlockSpec((256, units), lambda i: (i, 0))
    turned_spec = pl.BlockSpec((2 * chans, 256), lambda i: (0, i))
    weight_spec = whole((2 * chans, units))
    act_grad, grad_turned = call(
        grad_in_body,
        (tiles_dev,),
        [smem(), row_block, row_block, weight_spec],
        [unit_rows, turned_spec],
        [sds((cells, units), F32), sds((2 * chans, cells), BF16)],
        [], 2400000000, 12000000, (info, branch_grad, other_grad, w_down),
    )

    conv_out, left = conv(features, near, far, one, two, dw_bias.reshape(1, chans), False)
    conv_own = conv_out.reshape(cells, chans)
    conv_other = across(conv_own)

    gain_row = ln_gain.reshape(1, 2 * chans)
    full_row = whole((1, 2 * chans))
    normed_turned, active, pre_grad, back_keep, back_send, sums, branch_keep, branch_send = call(
        mlp_body,
        (tiles_dev,),
        [smem(), row_block, row_block, full_row, full_row, weight_spec, whole((1, units)), weight_spec, unit_rows],
        [turned_spec, unit_rows, unit_rows, row_block, row_block, pl.BlockSpec((256, LANES), lambda i: (i, 0)), row_block, row_block],
        [
            sds((2 * chans, cells), BF16), sds((cells, units), BF16), sds((cells, units), BF16),
            sds((cells, chans), F32), sds((cells, chans), BF16), sds((cells, LANES), F32),
            sds((cells, chans), F32), sds((cells, chans), BF16),
        ],
        [], 7200000000, 25000000,
        (info, conv_own, conv_other, gain_row, ln_bias.reshape(1, 2 * chans), w_up, up_bias.reshape(1, units), w_down, act_grad),
    )
    back_got = across(back_send)
    sums_got = across(sums)
    branch_got = across(branch_send)

    def outer(turned, right):
        return call(
            outer_body,
            (3,),
            [whole((2 * chans, cells)), pl.BlockSpec((cells, units // 3), lambda i: (0, i))],
            pl.BlockSpec((2 * chans, units // 3), lambda i: (0, i)),
            sds((2 * chans, units), BF16),
            [], 2400000000, 8000000, (turned, right),
        )

    grad_scale = lax.rsqrt(F32(side * side) * jnp.sum(tissue_count).astype(F32))

    def scattered(value):
        if devices & (devices - 1):
            return lax.psum_scatter(value.astype(F32), "space", scatter_dimension=0, tiled=True) * grad_scale
        value = value.reshape(devices, -1, units)
        bit = 1
        while bit < devices:
            halves = value.reshape(-1, 2, *value.shape[1:])
            high = (me // bit) % 2 == 1
            send = jnp.where(high, halves[:, 0], halves[:, 1])
            keep = jnp.where(high, halves[:, 1], halves[:, 0])
            got = lax.ppermute(send, "space", [(d, d ^ bit) for d in range(devices)])
            value = keep.astype(F32) + got.astype(F32)
            bit *= 2
            if bit < devices:
                value = value.astype(BF16)
        return value.reshape(-1, units) * grad_scale

    grad_down = scattered(outer(grad_turned, active))
    grad_up = scattered(outer(normed_turned, pre_grad))

    my_gain = lax.dynamic_slice_in_dim(gain_row, tensor_index * chans, chans, 1)
    sums_spec = pl.BlockSpec((256, LANES), lambda i: (i, 0))
    conv_grad, near_send, far_send = call(
        norm_back_body,
        (tiles_dev,),
        [smem(), row_block, row_block, row_block, row_block, sums_spec, sums_spec, whole((1, chans))],
        [row_block, whole(rim_shape), whole(rim_shape)],
        [sds((cells, chans), BF16), sds(rim_shape, BF16), sds(rim_shape, BF16)],
        [], 10000000, 6000000,
        (info, conv_own, conv_other, back_keep, back_got, sums, sums_got, my_gain),
    )
    near = paired(near_send, True, 0)
    far = paired(far_send, True, 1)
    conv_grad_tiles = conv_grad.reshape(features.shape)
    one_send, two_send = sides(conv_grad_tiles, near, far, False)
    one = paired(one_send, False, 0)
    two = paired(two_send, False, 1)
    taps = call(
        taps_body,
        (blocks,),
        [split_spec, pl.BlockSpec((1, 608, 1792), lambda c: (c, 0, 0))],
        pl.BlockSpec((56, LANES), lambda c: (0, c)),
        sds((56, chans), F32),
        [pltpu.VMEM((16, 32, 256), F32)], 5600000000, 9000000,
        (conv_grad.reshape(split_shape), left),
    )
    if devices & (devices - 1):
        taps = lax.psum(taps, "space")
    else:
        bit = 1
        while bit < devices:
            taps = taps + lax.ppermute(taps, "space", [(d, d ^ bit) for d in range(devices)])
            bit *= 2
    grad_kernel = taps[: KERNEL * KERNEL] * grad_scale

    tile_ok = (jnp.arange(tiles_dev, dtype=jnp.int32) < count).astype(F32)
    row_ok = jnp.repeat(tile_ok, side * side)[:, None]
    branch = branch_keep + branch_got.astype(F32) + down_bias
    block_out = ((features.reshape(cells, chans).astype(F32) + layer_scale * branch) * row_ok).astype(BF16)
    block_out = block_out.reshape(features.shape)

    (grad_features,) = conv(
        conv_grad_tiles, near, far, one, two, cotangent.reshape(split_shape), True
    )
    grad_features = grad_features.reshape(features.shape)
    return (block_out, grad_features, grad_up, grad_down, grad_kernel)


def solution(mesh):
    return jax.shard_map(
        on_device,
        mesh=mesh,
        in_specs=(
            P(("slide", "space"), None, None, "tensor"),
            P(None, "tensor"),
            P("tensor"),
            P(),
            P(),
            P(None, "tensor"),
            P("tensor"),
            P(None, "tensor"),
            P("tensor"),
            P("tensor"),
            P(("slide", "space"), None, None, "tensor"),
            P("slide", None),
            P("slide"),
        ),
        out_specs=(
            P(("slide", "space"), None, None, "tensor"),
            P(("slide", "space"), None, None, "tensor"),
            P(("slide", "space"), "tensor"),
            P(("slide", "space"), "tensor"),
            P("slide", "tensor"),
        ),
        check_vma=False,
    )
```

```python
import functools
import math

import jax
import jax.numpy as jnp
from jax import lax
from jax.experimental import pallas as pl
from jax.experimental.pallas import tpu as pltpu
from jax.sharding import PartitionSpec as P

KERNEL = 7
RIM = 3
LANES = 128
F32 = jnp.float32
BF16 = jnp.bfloat16
VMEM_BYTES = 12 * 1024 * 1024
CONV_BYTES = 24 * 1024 * 1024
CHUNKS = 3

TAIL_P = 0.39
TAIL = (
    0.2353252521737435,
    0.0913882086982987,
    0.6495599070595628,
    -0.635400901941762,
    0.8866647490628095,
    -0.2275372167464003,
)
ROOT_HALF = 0.7071067811865476
DENSITY = 0.3989422804014327


def smem():
    return pl.BlockSpec(memory_space=pltpu.SMEM)


def whole(shape):
    return pl.BlockSpec(shape, lambda *_: (0,) * len(shape))


class Chain:
    def __init__(self):
        self.token = None

    def __call__(self, body, grid, ins, outs, shapes, scratch, args, limit=VMEM_BYTES, nbytes=1000):
        label = getattr(body, "func", body).__name__.removesuffix("_body")
        first = [] if self.token is None else [self.token]
        n_in, n_out = len(args), len(outs)

        def run(*refs):
            refs = refs[len(first) :]
            body(*refs[: n_in + n_out], *refs[n_in + n_out + 1 :])

        *got, self.token = pl.pallas_call(
            run,
            grid=grid,
            in_specs=[pl.BlockSpec(memory_space=pl.ANY)] * len(first) + list(ins),
            out_specs=list(outs) + [whole((8, LANES))],
            out_shape=list(shapes) + [jax.ShapeDtypeStruct((8, LANES), F32)],
            name=label,
            scratch_shapes=scratch,
            compiler_params=pltpu.CompilerParams(vmem_limit_bytes=limit),
            cost_estimate=pl.CostEstimate(flops=nbytes * 100, bytes_accessed=nbytes, transcendentals=0),
        )(*first, *args)
        return got


def phi_pair(h):
    e = jnp.exp(h * h * -0.5)
    den = 1.0 + (TAIL_P * ROOT_HALF) * jnp.abs(h)
    t = pl.reciprocal(den, approx=True)
    t = t * (2.0 - den * t)
    acc = jnp.full_like(h, 0.5 * TAIL[5])
    for coef in TAIL[4::-1]:
        acc = acc * t + 0.5 * coef
    tail = acc * t * e
    return jnp.where(h >= 0, 1.0 - tail, tail), e


def place(cols, tissue_ref):
    me = lax.axis_index("space")
    return (me // cols) % 2, (me % cols) % 2, tissue_ref[me]


def store_rims(odd_row, top, bottom, near_ref, far_ref):
    @pl.when(odd_row == 0)
    def _():
        for side in range(2):
            near_ref[:, side * 16 : side * 16 + 16, :] = bottom[side]
            far_ref[:, side * 16 : side * 16 + 16, :] = top[side]

    @pl.when(odd_row == 1)
    def _():
        for side in range(2):
            near_ref[:, side * 16 : side * 16 + 16, :] = top[side]
            far_ref[:, side * 16 : side * 16 + 16, :] = bottom[side]


def rims_body(cols, tissue_ref, x_ref, cot_ref, scale_ref, near_ref, far_ref, grad_ref):
    odd_row, _, count = place(cols, tissue_ref)

    def masked(slot, lo, hi):
        return (x_ref[slot, lo:hi].astype(F32) * (slot < count).astype(F32)).astype(BF16)

    store_rims(
        odd_row,
        [masked(0, 0, 3), masked(1, 0, 3)],
        [masked(2, 13, 16), masked(3, 13, 16)],
        near_ref,
        far_ref,
    )
    scale = scale_ref[...].reshape(1, -1)
    for slot in range(4):
        rows = slice(slot * 256, slot * 256 + 256)
        ok = (slot < count).astype(F32)
        grad_ref[rows, :] = (cot_ref[rows, :].astype(F32) * (ok * scale)).astype(BF16)


def side_body(masked, cols, tissue_ref, x_ref, near_ref, far_ref, a_ref, b_ref, east, west, packed):
    odd_row, odd_col, count = place(cols, tissue_ref)
    for slot in range(4):
        value = x_ref[slot].astype(F32)
        if masked:
            value = value * (slot < count).astype(F32)
        rows = slice(RIM + (slot // 2) * 16, RIM + (slot // 2) * 16 + 16)
        if slot % 2:
            east[rows] = value[:, 8:16, :]
        else:
            west[rows] = value[:, 0:8, :]
    near = near_ref[...].astype(F32)
    far = far_ref[...].astype(F32)
    is_odd = (odd_row == 1).astype(F32)
    north = near * is_odd + far * (1.0 - is_odd)
    south = near * (1.0 - is_odd) + far * is_odd
    east[0:3] = north[:, 24:32, :]
    west[0:3] = north[:, 0:8, :]
    east[35:38] = south[:, 24:32, :]
    west[35:38] = south[:, 0:8, :]
    zero = jnp.zeros_like(east[38:40])
    east[38:40] = zero
    west[38:40] = zero

    def pack(out_ref, source, at):
        packed[:, 0:4, :] = source[0:20, at : at + 4, :]
        packed[:, 4:8, :] = source[20:40, at : at + 4, :]
        out_ref[...] = packed[...].reshape(out_ref.shape).astype(BF16)

    @pl.when(odd_col == 0)
    def _():
        pack(a_ref, east, 4)
        pack(b_ref, west, 0)

    @pl.when(odd_col == 1)
    def _():
        pack(a_ref, west, 0)
        pack(b_ref, east, 4)


def conv_body(backward, cols, tissue_ref, x_ref, near_ref, far_ref, a_ref, b_ref, w_ref, last_ref, out_ref, *rest):
    blocks = x_ref.shape[3] // LANES
    if backward:
        image, *scratch = rest
        lefts = [ref.at[0] for ref in scratch[:2]]
        lefts = [lefts[c % 2] for c in range(blocks)]
        scratch = scratch[2:]
    else:
        left_ref, image, *scratch = rest
        lefts = [left_ref.at[c] for c in range(blocks)]
    weights = [scratch[c % 2] for c in range(blocks)]
    odd_row, odd_col, count = place(cols, tissue_ref)
    row_odd = (odd_row == 1).astype(F32)
    col_odd = (odd_col == 1).astype(F32)
    eye = lax.broadcasted_iota(jnp.int32, (LANES, LANES), 0) == lax.broadcasted_iota(
        jnp.int32, (LANES, LANES), 1
    )
    empty = jnp.zeros((LANES, LANES), BF16)

    def fill(c):
        lanes = slice(c * LANES, (c + 1) * LANES)
        for slot in range(4):
            value = x_ref[slot, :, :, lanes].astype(F32)
            if not backward:
                value = value * (slot < count).astype(F32)
            r, q = slot // 2, slot % 2
            image[RIM + 16 * r : RIM + 16 * r + 16, 8 + 16 * q : 24 + 16 * q, :] = value
        near = near_ref[:, :, lanes].astype(F32)
        far = far_ref[:, :, lanes].astype(F32)
        image[0:3, 8:40, :] = near * row_odd + far * (1.0 - row_odd)
        image[35:38, 8:40, :] = near * (1.0 - row_odd) + far * row_odd
        first = a_ref[:, lanes].astype(F32).reshape(20, 8, LANES)
        second = b_ref[:, lanes].astype(F32).reshape(20, 8, LANES)
        from_left = first * col_odd + second * (1.0 - col_odd)
        from_right = first * (1.0 - col_odd) + second * col_odd
        image[20:40, 0:8, :] = from_left
        image[0:20, 4:8, :] = from_left[:, 0:4, :]
        image[0:20, 40:48, :] = from_right
        image[20:40, 40:44, :] = from_right[:, 4:8, :]

    def windows(c, b):
        value = image[0:38, 5 + b : 37 + b, :].astype(BF16).reshape(19, 2, 32, LANES)
        for par in range(2):
            at = b * 256 + par * LANES
            lefts[c][:, at : at + LANES] = value[:, par].reshape(608, LANES)

    def diagonals(c, b):
        lanes = slice(c * LANES, (c + 1) * LANES)
        for a in range(-1, KERNEL + 1):
            if 0 <= a < KERNEL:
                tap = (KERNEL - 1 - a) * KERNEL + KERNEL - 1 - b if backward else a * KERNEL + b
                block = jnp.where(eye, w_ref[tap : tap + 1, lanes], 0.0).astype(BF16)
            elif c < 2:
                block = empty
            else:
                continue
            for o in range(2):
                r = a + o
                if 0 <= r < 8:
                    at = (r // 2) * 1792 + b * 256 + (r % 2) * LANES
                    weights[c][at : at + LANES, o * LANES : (o + 1) * LANES] = block

    def product(c, q):
        return jnp.dot(
            lefts[c][32 * q : 32 * q + 512, :],
            weights[c][1792 * q : 1792 * (q + 1), :],
            preferred_element_type=F32,
        )

    def finish(c, acc):
        lanes = slice(c * LANES, (c + 1) * LANES)
        acc = acc.reshape(16, 32, 256)
        for slot in range(4):
            r, q = slot // 2, slot % 2
            for o in range(2):
                value = acc[8 * r : 8 * r + 8, 16 * q : 16 * q + 16, o * LANES : (o + 1) * LANES]
                if backward:
                    value = (value + last_ref[slot, :, o, :, lanes].astype(F32)) * (slot < count).astype(F32)
                else:
                    value = value + last_ref[:, lanes].reshape(1, 1, LANES)
                out_ref[slot, :, o, :, lanes] = value.astype(BF16)

    for c in range(blocks + 1):
        acc = None
        if c < blocks:
            fill(c)
        for q in range(4):
            if c:
                term = product(c - 1, q)
                acc = term if acc is None else acc + term
            if c < blocks:
                for b in range(2 * q, min(2 * q + 2, KERNEL)):
                    windows(c, b)
                    diagonals(c, b)
        if c:
            finish(c - 1, acc)


def taps_body(g_ref, left_ref, out_ref, paired, sums):
    for slot in range(4):
        r, q = slot // 2, slot % 2
        for o in range(2):
            paired[8 * r : 8 * r + 8, 16 * q : 16 * q + 16, o * LANES : (o + 1) * LANES] = g_ref[slot, :, o].astype(F32)
    turned = paired[...].reshape(512, 256).T.astype(BF16)
    group = lax.broadcasted_iota(jnp.int32, (8, LANES), 1) // 8
    place_in = lax.broadcasted_iota(jnp.int32, (8, LANES), 1) % 8 == lax.broadcasted_iota(jnp.int32, (8, LANES), 0)

    def product(q):
        return jnp.dot(turned, left_ref[0, 32 * q : 32 * q + 512, :], preferred_element_type=F32)

    def diagonals(q, prod):
        for b in range(KERNEL):
            for par in range(2):
                for o in range(2):
                    a = 2 * q + par - o
                    if not 0 <= a < KERNEL:
                        continue
                    cols = slice(b * 256 + par * LANES, b * 256 + (par + 1) * LANES)
                    value = prod[o * LANES : o * LANES + 8, cols]
                    for k in range(1, 16):
                        row = o * LANES + 8 * k
                        value = jnp.where(group == k, prod[row : row + 8, cols], value)
                    key = a * KERNEL + b
                    if o == 0:
                        sums[key] = value
                    else:
                        sums[key] = sums[key] + value

    ahead = product(0)
    for q in range(4):
        prod = ahead
        if q < 3:
            ahead = product(q + 1)
        diagonals(q, prod)
    total = jnp.sum(jnp.where(place_in[None], sums[...], 0.0), axis=1)
    out_ref[0:49, :] = total
    out_ref[49:64, :] = jnp.zeros((15, LANES), F32)


def pick(second, own, other):
    s = second.astype(F32)
    own = own.astype(F32)
    other = other.astype(F32)
    low = own * (1.0 - s) + other * s
    high = own * s + other * (1.0 - s)
    return jnp.concatenate([low, high], axis=1)


def store_turned(devices, out_ref, turned, cols):
    per = turned.shape[0] // devices
    if per % 16:
        out_ref[:, cols] = turned
        return
    odd = lax.axis_index("space") % 2
    half = turned.shape[0] // 2
    for d in range(devices):
        at = (d // 2) * per + jnp.where(odd == d % 2, 0, half)
        out_ref[pl.ds(pl.multiple_of(at, 16), per), cols] = turned[d * per : (d + 1) * per]


def grad_in_body(devices, own_ref, other_ref, w_ref, out_ref, turned_ref, full_ref):
    second = lax.axis_index("tensor") == 1
    for slot in range(4):
        rows = slice(slot * 256, slot * 256 + 256)
        full = pick(second, own_ref[rows, :], other_ref[rows, :]).astype(BF16)
        full_ref[rows, :] = full
        store_turned(devices, turned_ref, full.T, rows)
        out_ref[rows, :] = jnp.dot(full, w_ref[...], preferred_element_type=F32)


def grad_more_body(full_ref, w_ref, out_ref):
    out_ref[...] = jnp.dot(full_ref[...], w_ref[...], preferred_element_type=F32)


def in_lanes(columns, lanes):
    lane = lax.broadcasted_iota(jnp.int32, (columns[0].shape[0], lanes), 1)
    value = jnp.zeros(lane.shape, F32)
    for at, column in enumerate(columns):
        value = jnp.where(lane == at, column, value)
    return value


def norm_body(devices, own_ref, other_ref, gain_ref, shift_ref, out_ref, turned_ref, stats_ref):
    gain = gain_ref[...].reshape(1, -1)
    shift = shift_ref[...].reshape(1, -1)
    second = lax.axis_index("tensor") == 1
    for slot in range(4):
        rows = slice(slot * 256, slot * 256 + 256)
        full = pick(second, own_ref[rows, :], other_ref[rows, :])
        mean = jnp.mean(full, axis=1, keepdims=True)
        centered = full - mean
        var = jnp.mean(centered * centered, axis=1, keepdims=True)
        inverse = lax.rsqrt(var + 1e-06)
        stats_ref[rows, :] = in_lanes((mean, inverse), stats_ref.shape[1])
        value = (centered * inverse * gain + shift).astype(BF16)
        out_ref[rows, :] = value
        store_turned(devices, turned_ref, value.T, rows)


def chunk_body(normed_ref, up_ref, bias_ref, in_ref, grad_turned_ref, turned_ref, act_ref, pre_ref, keep_ref, send_ref):
    bias = bias_ref[...]
    half = keep_ref.shape[1]
    for slot in range(4):
        rows = slice(slot * 256, slot * 256 + 256)
        hidden = jnp.dot(normed_ref[rows, :], up_ref[...], preferred_element_type=F32) + bias
        phi, e = phi_pair(hidden)
        act_ref[rows, :] = (hidden * phi).astype(BF16)
        pre_ref[rows, :] = (in_ref[rows, :] * (phi + hidden * (e * DENSITY))).astype(BF16)
    for at, left, right in ((0, grad_turned_ref, act_ref), (1, turned_ref, pre_ref)):
        grad = jnp.dot(left[...], right[...], preferred_element_type=F32).astype(BF16)
        keep_ref[at] = grad[:half]
        send_ref[at] = grad[half:]


def split(second, value):
    half = value.shape[1] // 2
    s = second.astype(F32)
    low, high = value[:, :half], value[:, half:]
    return low * (1.0 - s) + high * s, low * s + high * (1.0 - s)


def turned_dot(values, w_ref):
    total = None
    for at, ref in enumerate(values):
        width = ref.shape[1]
        term = lax.dot_general(
            ref[...], w_ref[:, at * width : (at + 1) * width], (((1,), (1,)), ((), ())), preferred_element_type=F32
        )
        total = term if total is None else total + term
    return total


def back_body(own_ref, other_ref, stats_ref, gain_ref, up_ref, *rest):
    pres, (keep_ref, send_ref, more_ref, sums_ref) = rest[:CHUNKS], rest[CHUNKS:]
    second = lax.axis_index("tensor") == 1
    back = turned_dot(pres, up_ref)
    rows = pick(second, own_ref[...], other_ref[...])
    stats = stats_ref[...]
    normalized = (rows - stats[:, 0:1]) * stats[:, 1:2]
    scaled = back * gain_ref[...].reshape(1, -1)
    both = (jnp.sum(scaled, axis=1, keepdims=True), jnp.sum(scaled * normalized, axis=1, keepdims=True))
    sums_ref[...] = in_lanes(both, LANES)
    pieces = []
    for value in both:
        for _ in range(3):
            piece = value.astype(BF16).astype(F32)
            pieces.append(piece)
            value = value - piece
    half = keep_ref.shape[1]
    keep, send = split(second, back)
    keep_ref[...] = keep
    cut = send_ref.shape[1]
    send_ref[...] = send[:, :cut].astype(BF16)
    more_ref[:, : half - cut] = send[:, cut:].astype(BF16)
    more_ref[:, half - cut :] = in_lanes(pieces, LANES).astype(BF16)


def branch_body(down_ref, *rest):
    acts, (keep_ref, send_ref, more_ref) = rest[:CHUNKS], rest[CHUNKS:]
    keep, send = split(lax.axis_index("tensor") == 1, turned_dot(acts, down_ref))
    keep_ref[...] = keep
    cut = send_ref.shape[1]
    send_ref[...] = send[:, :cut].astype(BF16)
    more_ref[...] = send[:, cut:].astype(BF16)


def first_body(keep_ref, got_ref, keep_out, send_out):
    bit = (lax.axis_index("space") // 2) % 2
    for half in range(2):
        for out_ref, at in ((keep_out, 2 * half + bit), (send_out, 2 * half + 1 - bit)):
            value = keep_ref[:, at].astype(F32) + got_ref[:, at].astype(F32)
            out_ref[:, half] = value.astype(out_ref.dtype)


def second_body(keep_ref, got_ref, keep_out, send_out):
    bit = lax.axis_index("space") // 4
    keep_out[...] = keep_ref[:, bit] + got_ref[:, bit].astype(F32)
    send_out[...] = (keep_ref[:, 1 - bit] + got_ref[:, 1 - bit].astype(F32)).astype(BF16)


def third_body(keep_ref, got_ref, out_ref):
    out_ref[...] = keep_ref[...] + got_ref[...].astype(F32)


def put_taps(value, send_ref, at):
    high = value.astype(BF16)
    low = (value - high.astype(F32)).astype(BF16)
    rows = value.shape[0]
    for lanes in range(value.shape[1] // LANES):
        cols = slice(lanes * LANES, (lanes + 1) * LANES)
        send_ref[at : at + rows, :] = high[:, cols]
        send_ref[at + rows : at + 2 * rows, :] = low[:, cols]
        at += 2 * rows
    return high.astype(F32) + low.astype(F32)


def got_taps(got_ref, at, shape):
    rows, width = shape
    parts = []
    for lanes in range(width // LANES):
        parts.append(got_ref[at : at + rows, :].astype(F32) + got_ref[at + rows : at + 2 * rows, :].astype(F32))
        at += 2 * rows
    return jnp.concatenate(parts, axis=1)


def first_taps_body(keep_ref, got_ref, taps_ref, taps_got_ref, keep_out, send_out, taps_out):
    bit = (lax.axis_index("space") // 2) % 2
    per, width = keep_ref.shape[2:]
    blocks = width // LANES
    for half in range(2):
        at = 2 * half + bit
        keep_out[:, half] = keep_ref[:, at].astype(F32) + got_ref[:, at].astype(F32)
        at = 2 * half + 1 - bit
        value = (keep_ref[:, at].astype(F32) + got_ref[:, at].astype(F32)).astype(BF16)
        for g in range(2):
            for lanes in range(blocks):
                row = ((g * 2 + half) * blocks + lanes) * per
                send_out[row : row + per, :] = value[g, :, lanes * LANES : (lanes + 1) * LANES]
    taps_out[...] = put_taps(taps_ref[...] + taps_got_ref[...], send_out, 4 * blocks * per)


def second_taps_body(keep_ref, got_ref, taps_ref, keep_out, send_out, taps_out):
    bit = lax.axis_index("space") // 4
    per, width = keep_ref.shape[2:]
    blocks = width // LANES
    for g in range(2):
        for lanes in range(blocks):
            cols = slice(lanes * LANES, (lanes + 1) * LANES)

            def got(half):
                row = pl.multiple_of(((g * 2 + half) * blocks + lanes) * per, 16)
                return got_ref[pl.ds(row, per), :].astype(F32)

            keep_out[g, :, cols] = keep_ref[g, bit, :, cols] + got(bit)
            row = (g * blocks + lanes) * per
            send_out[row : row + per, :] = (keep_ref[g, 1 - bit, :, cols] + got(1 - bit)).astype(BF16)
    total = taps_ref[...] + got_taps(got_ref, 4 * blocks * per, taps_ref.shape)
    taps_out[...] = put_taps(total, send_out, 2 * blocks * per)


def last_body(tissue_ref, *refs):
    *sums, keep_ref, got_ref, taps_ref, down_ref, up_ref, kernel_ref = refs
    tiles = tissue_ref[0]
    for at in range(1, tissue_ref.shape[0]):
        tiles = tiles + tissue_ref[at]
    scale = lax.rsqrt(jnp.full((8, LANES), 256.0, F32) * tiles.astype(F32))[0:1, 0:1]
    per, width = keep_ref.shape[1:]
    blocks = width // LANES
    for at, out_ref in enumerate((down_ref, up_ref)):
        for k, ref in enumerate(sums):
            out_ref[:, k * width : (k + 1) * width] = ref[at] * scale
        for lanes in range(blocks):
            cols = slice(lanes * LANES, (lanes + 1) * LANES)
            row = (at * blocks + lanes) * per
            value = keep_ref[at, :, cols] + got_ref[row : row + per, :].astype(F32)
            start = len(sums) * width + lanes * LANES
            out_ref[:, start : start + LANES] = value * scale
    total = taps_ref[...] + got_taps(got_ref, 2 * blocks * per, taps_ref.shape)
    kernel_ref[...] = (total * scale)[: kernel_ref.shape[0]]


def block_out_body(tissue_ref, x_ref, keep_ref, got_ref, more_ref, scale_ref, bias_ref, out_ref):
    count = tissue_ref[lax.axis_index("space")]
    ok = (pl.program_id(0) < count).astype(F32)
    got = jnp.concatenate([got_ref[...], more_ref[...]], axis=1).astype(F32)
    branch = keep_ref[...] + got + bias_ref[...].reshape(1, -1)
    value = (x_ref[...].astype(F32) + scale_ref[...].reshape(1, -1) * branch) * ok
    out_ref[...] = value.astype(BF16)


def norm_back_body(cols, tissue_ref, own_ref, stats_ref, keep_ref, got_ref, more_ref, sums_ref, gain_ref, out_ref, near_ref, far_ref):
    half = own_ref.shape[1]
    stats = stats_ref[...]
    inverse = stats[:, 1:2]
    normalized = (own_ref[...].astype(F32) - stats[:, 0:1]) * inverse
    got = jnp.concatenate([got_ref[...], more_ref[...]], axis=1).astype(F32)
    scaled = (keep_ref[...] + got[:, :half]) * gain_ref[...]
    sums = sums_ref[...]
    first = (sums[:, 0:1] + (got[:, half : half + 1] + got[:, half + 1 : half + 2] + got[:, half + 2 : half + 3])) / (2.0 * half)
    other = (sums[:, 1:2] + (got[:, half + 3 : half + 4] + got[:, half + 4 : half + 5] + got[:, half + 5 : half + 6])) / (2.0 * half)
    grad = inverse * (scaled - first - normalized * other)
    out_ref[...] = grad.astype(BF16)
    tile = grad.reshape(16, 16, grad.shape[1])
    odd_row, _, _ = place(cols, tissue_ref)
    slot = pl.program_id(0)
    for side in range(2):
        span = slice(side * 16, side * 16 + 16)

        @pl.when(slot == side)
        def _():
            top = tile[0:3].astype(BF16)

            @pl.when(odd_row == 0)
            def _():
                far_ref[:, span, :] = top

            @pl.when(odd_row == 1)
            def _():
                near_ref[:, span, :] = top

        @pl.when(slot == side + 2)
        def _():
            bottom = tile[13:16].astype(BF16)

            @pl.when(odd_row == 0)
            def _():
                near_ref[:, span, :] = bottom

            @pl.when(odd_row == 1)
            def _():
                far_ref[:, span, :] = bottom


def on_device(
    features, dw_kernel, dw_bias, ln_gain, ln_bias, w_up, up_bias, w_down, down_bias, layer_scale,
    cotangent, neighbors, tissue_count,
):
    tiles_dev, side, _, chans = features.shape
    units = w_up.shape[1]
    cells = tiles_dev * side * side
    devices = lax.axis_size("space")
    me = lax.axis_index("space")
    tensor_index = lax.axis_index("tensor")
    block_rows = max(d for d in range(1, math.isqrt(devices) + 1) if devices % d == 0)
    block_cols = devices // block_rows
    blocks = chans // LANES

    call = Chain()

    def sds(shape, dtype):
        return jax.ShapeDtypeStruct(shape, dtype)

    hbm = pltpu.HBM

    def pin(value):
        return pltpu.with_memory_space_constraint(value, pltpu.HBM)

    def across(value):
        return lax.ppermute(value, "tensor", [(0, 1), (1, 0)])

    def exchanged(value, bit):
        return lax.ppermute(value, "space", [(d, d ^ bit) for d in range(devices)])

    def paired(value, along_rows, round_at):
        size = block_rows if along_rows else block_cols
        pairs = []
        for d in range(devices):
            place = d // block_cols if along_rows else d % block_cols
            other = place + 1 if place % 2 == round_at else place - 1
            if 0 <= other < size:
                pairs.append((d, d + (other - place) * (block_cols if along_rows else 1)))
        if not pairs:
            return jnp.zeros_like(value)
        return lax.ppermute(value, "space", pairs)

    rim_shape = (RIM, 2 * side, chans)
    pack_shape = (160, chans)

    def sides(x, near, far, masked):
        return call(
            functools.partial(side_body, masked, block_cols),
            (1,),
            [smem(), whole(features.shape), whole(rim_shape), whole(rim_shape)],
            [whole(pack_shape)] * 2,
            [sds(pack_shape, BF16)] * 2,
            [pltpu.VMEM((40, 8, chans), F32), pltpu.VMEM((40, 8, chans), F32), pltpu.VMEM((20, 8, chans), F32)],
            (tissue, x, near, far),
        )

    split_shape = (4, 8, 2, side, chans)
    split_spec = pl.BlockSpec((4, 8, 2, side, LANES), lambda c: (0, 0, 0, 0, c))

    left_shape = (blocks, 608, 1792)

    def conv(x, near, far, one, two, last, backward):
        outs = [whole(split_shape)]
        shapes = [sds(split_shape, BF16)]
        scratch = [pltpu.VMEM((40, 48, LANES), F32)]
        if backward:
            scratch += [pltpu.VMEM((1,) + left_shape[1:], BF16)] * 2
        else:
            outs.append(whole(left_shape))
            shapes.append(hbm(left_shape, BF16))
        scratch += [pltpu.VMEM((4 * 1792, 256), BF16)] * 2
        return call(
            functools.partial(conv_body, backward, block_cols),
            (1,),
            [
                smem(), whole(features.shape), whole(rim_shape), whole(rim_shape), whole(pack_shape), whole(pack_shape),
                whole((KERNEL * KERNEL, chans)), whole(last.shape),
            ],
            outs, shapes, scratch,
            (tissue, x, near, far, one, two, dw_kernel, last), CONV_BYTES, 100000000 if backward else 1000,
        )

    total = 2 * chans
    width = units // CHUNKS

    def at_chunk(shape, k):
        return pl.BlockSpec(shape, lambda *_: (0, k))

    tissue = pin(tissue_count)
    near_send, far_send, branch_grad = call(
        functools.partial(rims_body, block_cols),
        (1,),
        [smem(), whole(features.shape), whole((cells, chans)), whole((chans,))],
        [whole(rim_shape), whole(rim_shape), whole((cells, chans))],
        [sds(rim_shape, BF16), sds(rim_shape, BF16), sds((cells, chans), BF16)],
        [], (tissue, pin(features), pin(cotangent.reshape(cells, chans)), layer_scale),
    )
    near = paired(near_send, True, 0)
    far = paired(far_send, True, 1)
    other_grad = across(branch_grad)
    act_grads = [None] * CHUNKS
    act_grads[0], grad_turned, grad_full = call(
        functools.partial(grad_in_body, devices),
        (1,),
        [whole((cells, chans)), whole((cells, chans)), at_chunk((total, width), 0)],
        [whole((cells, width)), whole((total, cells)), whole((cells, total))],
        [sds((cells, width), F32), sds((total, cells), BF16), sds((cells, total), BF16)],
        [], (branch_grad, other_grad, w_down),
    )
    one_send, two_send = sides(features, near, far, True)
    one = paired(one_send, False, 0)
    two = paired(two_send, False, 1)

    def more(k):
        (act_grads[k],) = call(
            grad_more_body,
            (1,),
            [whole((cells, total)), at_chunk((total, width), k)],
            [whole((cells, width))],
            [sds((cells, width), F32)],
            [], (grad_full, w_down),
        )

    for k in range(1, CHUNKS - 1):
        more(k)
    conv_out, left = conv(features, near, far, one, two, dw_bias.reshape(1, chans), False)
    conv_own = conv_out.reshape(cells, chans)
    conv_other = across(conv_own)
    more(CHUNKS - 1)
    normed, normed_turned, stats = call(
        functools.partial(norm_body, devices),
        (1,),
        [whole((cells, chans)), whole((cells, chans)), whole((total,)), whole((total,))],
        [whole((cells, total)), whole((total, cells)), whole((cells, LANES))],
        [sds((cells, total), BF16), sds((total, cells), BF16), sds((cells, LANES), F32)],
        [], (conv_own, conv_other, ln_gain, ln_bias),
    )

    grad_scale = lax.rsqrt(F32(side * side) * jnp.sum(tissue_count).astype(F32))
    stepped = devices == 8
    per = total // devices
    acts, pres, kept, got = [], [], [], []
    for k in range(CHUNKS):
        act, pre, keep, send = call(
            chunk_body,
            (1,),
            [
                whole((cells, total)), at_chunk((total, width), k), at_chunk((1, width), k), whole((cells, width)),
                whole((total, cells)), whole((total, cells)),
            ],
            [whole((cells, width)), whole((cells, width)), whole((2, chans, width)), whole((2, chans, width))],
            [hbm((cells, width), BF16), sds((cells, width), BF16), sds((2, chans, width), BF16), hbm((2, chans, width), BF16)],
            [],
            (normed, w_up, up_bias.reshape(1, units), act_grads[k], grad_turned, normed_turned),
        )
        acts.append(act)
        pres.append(pre)
        kept.append(keep)
        got.append(exchanged(send, 1) if stepped else send)

    def first(k):
        if stepped:
            shape = (2, 4, per, width)
            out = (2, 2, per, width)
            keep, send = call(
                first_body, (1,), [whole(shape)] * 2, [whole(out)] * 2, [hbm(out, F32), sds(out, BF16)], [],
                (kept[k].reshape(shape), got[k].reshape(shape)),
            )
            kept[k], got[k] = keep, exchanged(send, 2)

    def second(k):
        if stepped:
            out = (2, per, width)
            keep, send = call(
                second_body, (1,), [whole((2, 2, per, width))] * 2, [whole(out)] * 2, [sds(out, F32), sds(out, BF16)], [],
                (pin(kept[k]), got[k]),
            )
            kept[k], got[k] = keep, exchanged(send, 4)

    def third(k):
        if stepped:
            out = (2, per, width)
            (kept[k],) = call(
                third_body, (1,), [whole(out)] * 2, [whole(out)], [sds(out, F32)], [], (kept[k], got[k])
            )

    def scattered(k):
        value = jnp.concatenate([kept[k], got[k]], axis=1)
        if devices & (devices - 1):
            return lax.psum_scatter(value.astype(F32), "space", scatter_dimension=1, tiled=True) * grad_scale
        value = value.reshape(2, devices, -1, width)
        bit = 1
        while bit < devices:
            halves = value.reshape(2, -1, 2, *value.shape[2:])
            high = (me // bit) % 2 == 1
            send = jnp.where(high, halves[:, :, 0], halves[:, :, 1])
            keep = jnp.where(high, halves[:, :, 1], halves[:, :, 0])
            value = keep.astype(F32) + exchanged(send, bit).astype(F32)
            bit *= 2
            if bit < devices:
                value = value.astype(BF16)
        return value.reshape(2, -1, width) * grad_scale

    row_block = pl.BlockSpec((256, chans), lambda i: (i, 0))
    sums_spec = pl.BlockSpec((256, LANES), lambda i: (i, 0))
    wide = (chans + LANES) // 2
    wide_block = pl.BlockSpec((256, wide), lambda i: (i, 0))
    chunk_rows = [pl.BlockSpec((256, width), lambda i: (i, 0))] * CHUNKS
    back_keep, back_send, back_more, sums = call(
        back_body,
        (tiles_dev,),
        [row_block, row_block, sums_spec, whole((total,)), whole((total, units))] + chunk_rows,
        [row_block, wide_block, wide_block, sums_spec],
        [hbm((cells, chans), F32), hbm((cells, wide), BF16), hbm((cells, wide), BF16), hbm((cells, LANES), F32)],
        [], (conv_own, conv_other, stats, ln_gain, w_up, *pres),
    )
    back_got = across(back_send), across(back_more)
    def first_taps(k):
        out = (2, 2, per, width)
        rows = 4 * per * width // LANES + 2 * taps.shape[0] * blocks
        shape = (2, 4, per, width)
        keep, send, value = call(
            first_taps_body, (1,), [whole(shape)] * 2 + [whole(taps.shape)] * 2,
            [whole(out), whole((rows, LANES)), whole(taps.shape)],
            [sds(out, F32), sds((rows, LANES), BF16), sds(taps.shape, F32)], [],
            (kept[k].reshape(shape), got[k].reshape(shape), taps, taps_got),
        )
        kept[k], got[k] = keep, exchanged(send, 2)
        return value

    def second_taps(k):
        out = (2, per, width)
        was = got[k].shape
        rows = 2 * per * width // LANES + 2 * taps.shape[0] * blocks
        keep, send, value = call(
            second_taps_body, (1,), [whole((2, 2, per, width)), whole(was), whole(taps.shape)],
            [whole(out), whole((rows, LANES)), whole(taps.shape)],
            [sds(out, F32), sds((rows, LANES), BF16), sds(taps.shape, F32)], [], (kept[k], got[k], taps),
        )
        kept[k], got[k] = keep, exchanged(send, 4)
        return value

    first(0)
    my_gain = lax.dynamic_slice_in_dim(ln_gain.reshape(1, total), lax.axis_index("tensor") * chans, chans, 1)
    conv_grad, near_send, far_send = call(
        functools.partial(norm_back_body, block_cols),
        (tiles_dev,),
        [smem(), row_block, sums_spec, row_block, wide_block, wide_block, sums_spec, whole((1, chans))],
        [row_block, whole(rim_shape), whole(rim_shape)],
        [sds((cells, chans), BF16), sds(rim_shape, BF16), sds(rim_shape, BF16)],
        [],
        (tissue, pin(conv_own), pin(stats), pin(back_keep), *back_got, pin(sums), my_gain),
    )
    near = paired(near_send, True, 0)
    far = paired(far_send, True, 1)
    branch_keep, branch_send, branch_more = call(
        branch_body,
        (tiles_dev,),
        [whole((total, units))] + chunk_rows,
        [row_block, pl.BlockSpec((256, 2 * LANES), lambda i: (i, 0)), sums_spec],
        [sds((cells, chans), F32), sds((cells, 2 * LANES), BF16), sds((cells, LANES), BF16)],
        [], (w_down, *acts),
    )
    branch_got = across(branch_send), across(branch_more)
    second(0)
    conv_grad_tiles = conv_grad.reshape(features.shape)
    one_send, two_send = sides(conv_grad_tiles, near, far, False)
    one = paired(one_send, False, 0)
    two = paired(two_send, False, 1)
    first(1)
    (taps,) = call(
        taps_body,
        (blocks,),
        [split_spec, pl.BlockSpec((1, 608, 1792), lambda c: (c, 0, 0))],
        [pl.BlockSpec((64, LANES), lambda c: (0, c))],
        [sds((64, chans), F32)],
        [pltpu.VMEM((16, 32, 256), F32), pltpu.VMEM((KERNEL * KERNEL, 8, LANES), F32)],
        (conv_grad.reshape(split_shape), pin(left)),
    )
    taps_got = exchanged(taps, 1) if stepped else None
    third(0)
    (block_out,) = call(
        block_out_body,
        (tiles_dev,),
        [smem(), row_block, row_block, pl.BlockSpec((256, 2 * LANES), lambda i: (i, 0)), sums_spec, whole((chans,)), whole((chans,))],
        [row_block],
        [sds((cells, chans), BF16)],
        [], (tissue, features.reshape(cells, chans), branch_keep, *branch_got, layer_scale, down_bias),
    )
    block_out = block_out.reshape(features.shape)
    second(1)
    if stepped:
        taps = first_taps(2)
    third(1)
    (grad_features,) = conv(
        conv_grad_tiles, near, far, one, two, cotangent.reshape(split_shape), True
    )
    grad_features = grad_features.reshape(features.shape)
    if stepped:
        taps = second_taps(2)
    if stepped:
        kernel_shape = (KERNEL * KERNEL, chans)
        grad_down, grad_up, grad_kernel = call(
            last_body,
            (1,),
            [smem()] + [whole((2, per, width))] * CHUNKS + [whole(got[CHUNKS - 1].shape), whole(taps.shape)],
            [whole((per, units))] * 2 + [whole(kernel_shape)],
            [sds((per, units), F32)] * 2 + [sds(kernel_shape, F32)],
            [], (tissue, *kept, got[CHUNKS - 1], taps),
        )
    else:
        grad_kernel = lax.psum(taps, "space")[: KERNEL * KERNEL] * grad_scale
        grads = [scattered(k) for k in range(CHUNKS)]
        grad_down = jnp.concatenate([g[0] for g in grads], axis=1).reshape(-1, units)
        grad_up = jnp.concatenate([g[1] for g in grads], axis=1).reshape(-1, units)
    return (block_out, grad_features, grad_up, grad_down, grad_kernel)


def solution(mesh):
    return jax.shard_map(
        on_device,
        mesh=mesh,
        in_specs=(
            P(("slide", "space"), None, None, "tensor"),
            P(None, "tensor"),
            P("tensor"),
            P(),
            P(),
            P(None, "tensor"),
            P("tensor"),
            P(None, "tensor"),
            P("tensor"),
            P("tensor"),
            P(("slide", "space"), None, None, "tensor"),
            P("slide", None),
            P("slide"),
        ),
        out_specs=(
            P(("slide", "space"), None, None, "tensor"),
            P(("slide", "space"), None, None, "tensor"),
            P(("slide", "space"), "tensor"),
            P(("slide", "space"), "tensor"),
            P("slide", "tensor"),
        ),
        check_vma=False,
    )
```

```python
import functools
import math

import jax
import jax.numpy as jnp
from jax import lax
from jax.experimental import pallas as pl
from jax.experimental.pallas import tpu as pltpu
from jax.sharding import PartitionSpec as P

KERNEL = 7
RIM = 3
LANES = 128
F32 = jnp.float32
BF16 = jnp.bfloat16
VMEM_BYTES = 12 * 1024 * 1024
CONV_BYTES = 24 * 1024 * 1024
CHUNKS = 3

TAIL_P = 0.39
TAIL = (
    0.2353252521737435,
    0.0913882086982987,
    0.6495599070595628,
    -0.635400901941762,
    0.8866647490628095,
    -0.2275372167464003,
)
ROOT_HALF = 0.7071067811865476
DENSITY = 0.3989422804014327


def smem():
    return pl.BlockSpec(memory_space=pltpu.SMEM)


def whole(shape):
    return pl.BlockSpec(shape, lambda *_: (0,) * len(shape))


class Chain:
    def __init__(self):
        self.token = None

    def __call__(self, body, grid, ins, outs, shapes, scratch, args, limit=VMEM_BYTES, nbytes=1000):
        label = getattr(body, "func", body).__name__.removesuffix("_body")
        first = [] if self.token is None else [self.token]
        n_in, n_out = len(args), len(outs)

        def run(*refs):
            refs = refs[len(first) :]
            body(*refs[: n_in + n_out], *refs[n_in + n_out + 1 :])

        *got, self.token = pl.pallas_call(
            run,
            grid=grid,
            in_specs=[pl.BlockSpec(memory_space=pl.ANY)] * len(first) + list(ins),
            out_specs=list(outs) + [whole((8, LANES))],
            out_shape=list(shapes) + [jax.ShapeDtypeStruct((8, LANES), F32)],
            name=label,
            scratch_shapes=scratch,
            compiler_params=pltpu.CompilerParams(vmem_limit_bytes=limit),
            cost_estimate=pl.CostEstimate(flops=nbytes * 100, bytes_accessed=nbytes, transcendentals=0),
        )(*first, *args)
        return got


def phi_pair(h):
    e = jnp.exp(h * h * -0.5)
    den = 1.0 + (TAIL_P * ROOT_HALF) * jnp.abs(h)
    t = pl.reciprocal(den, approx=True)
    t = t * (2.0 - den * t)
    acc = jnp.full_like(h, 0.5 * TAIL[5])
    for coef in TAIL[4::-1]:
        acc = acc * t + 0.5 * coef
    tail = acc * t * e
    return jnp.where(h >= 0, 1.0 - tail, tail), e


def place(cols, tissue_ref):
    me = lax.axis_index("space")
    return (me // cols) % 2, (me % cols) % 2, tissue_ref[me]


def store_rims(odd_row, top, bottom, near_ref, far_ref):
    @pl.when(odd_row == 0)
    def _():
        for side in range(2):
            near_ref[:, side * 16 : side * 16 + 16, :] = bottom[side]
            far_ref[:, side * 16 : side * 16 + 16, :] = top[side]

    @pl.when(odd_row == 1)
    def _():
        for side in range(2):
            near_ref[:, side * 16 : side * 16 + 16, :] = top[side]
            far_ref[:, side * 16 : side * 16 + 16, :] = bottom[side]


def rims_body(cols, tissue_ref, x_ref, cot_ref, scale_ref, near_ref, far_ref, grad_ref):
    odd_row, _, count = place(cols, tissue_ref)

    def masked(slot, lo, hi):
        return (x_ref[slot, lo:hi].astype(F32) * (slot < count).astype(F32)).astype(BF16)

    store_rims(
        odd_row,
        [masked(0, 0, 3), masked(1, 0, 3)],
        [masked(2, 13, 16), masked(3, 13, 16)],
        near_ref,
        far_ref,
    )
    scale = scale_ref[...].reshape(1, -1)
    for slot in range(4):
        rows = slice(slot * 256, slot * 256 + 256)
        ok = (slot < count).astype(F32)
        grad_ref[rows, :] = (cot_ref[rows, :].astype(F32) * (ok * scale)).astype(BF16)


def side_body(masked, cols, tissue_ref, x_ref, near_ref, far_ref, a_ref, b_ref, east, west, packed):
    odd_row, odd_col, count = place(cols, tissue_ref)
    for slot in range(4):
        value = x_ref[slot].astype(F32)
        if masked:
            value = value * (slot < count).astype(F32)
        rows = slice(RIM + (slot // 2) * 16, RIM + (slot // 2) * 16 + 16)
        if slot % 2:
            east[rows] = value[:, 8:16, :]
        else:
            west[rows] = value[:, 0:8, :]
    near = near_ref[...].astype(F32)
    far = far_ref[...].astype(F32)
    is_odd = (odd_row == 1).astype(F32)
    north = near * is_odd + far * (1.0 - is_odd)
    south = near * (1.0 - is_odd) + far * is_odd
    east[0:3] = north[:, 24:32, :]
    west[0:3] = north[:, 0:8, :]
    east[35:38] = south[:, 24:32, :]
    west[35:38] = south[:, 0:8, :]
    zero = jnp.zeros_like(east[38:40])
    east[38:40] = zero
    west[38:40] = zero

    def pack(out_ref, source, at):
        packed[:, 0:4, :] = source[0:20, at : at + 4, :]
        packed[:, 4:8, :] = source[20:40, at : at + 4, :]
        out_ref[...] = packed[...].reshape(out_ref.shape).astype(BF16)

    @pl.when(odd_col == 0)
    def _():
        pack(a_ref, east, 4)
        pack(b_ref, west, 0)

    @pl.when(odd_col == 1)
    def _():
        pack(a_ref, west, 0)
        pack(b_ref, east, 4)


def conv_body(backward, cols, tissue_ref, x_ref, near_ref, far_ref, a_ref, b_ref, w_ref, last_ref, out_ref, *rest):
    blocks = x_ref.shape[3] // LANES
    if backward:
        image, *scratch = rest
        lefts = [ref.at[0] for ref in scratch[:2]]
        lefts = [lefts[c % 2] for c in range(blocks)]
        scratch = scratch[2:]
    else:
        left_ref, image, windows_ref, sems, *scratch = rest
        lefts = [windows_ref.at[c] for c in range(blocks)]
        copies = [pltpu.make_async_copy(lefts[c], left_ref.at[c], sems.at[c]) for c in range(blocks)]
    weights = [scratch[c % 2] for c in range(blocks)]
    odd_row, odd_col, count = place(cols, tissue_ref)
    row_odd = (odd_row == 1).astype(F32)
    col_odd = (odd_col == 1).astype(F32)
    eye = lax.broadcasted_iota(jnp.int32, (LANES, LANES), 0) == lax.broadcasted_iota(
        jnp.int32, (LANES, LANES), 1
    )
    empty = jnp.zeros((LANES, LANES), BF16)

    def fill(c):
        lanes = slice(c * LANES, (c + 1) * LANES)
        for slot in range(4):
            value = x_ref[slot, :, :, lanes].astype(F32)
            if not backward:
                value = value * (slot < count).astype(F32)
            r, q = slot // 2, slot % 2
            image[RIM + 16 * r : RIM + 16 * r + 16, 8 + 16 * q : 24 + 16 * q, :] = value
        near = near_ref[:, :, lanes].astype(F32)
        far = far_ref[:, :, lanes].astype(F32)
        image[0:3, 8:40, :] = near * row_odd + far * (1.0 - row_odd)
        image[35:38, 8:40, :] = near * (1.0 - row_odd) + far * row_odd
        first = a_ref[:, lanes].astype(F32).reshape(20, 8, LANES)
        second = b_ref[:, lanes].astype(F32).reshape(20, 8, LANES)
        from_left = first * col_odd + second * (1.0 - col_odd)
        from_right = first * (1.0 - col_odd) + second * col_odd
        image[20:40, 0:8, :] = from_left
        image[0:20, 4:8, :] = from_left[:, 0:4, :]
        image[0:20, 40:48, :] = from_right
        image[20:40, 40:44, :] = from_right[:, 4:8, :]

    def windows(c, b):
        value = image[0:38, 5 + b : 37 + b, :].astype(BF16).reshape(19, 2, 32, LANES)
        for par in range(2):
            at = b * 256 + par * LANES
            lefts[c][:, at : at + LANES] = value[:, par].reshape(608, LANES)

    def diagonals(c, b):
        lanes = slice(c * LANES, (c + 1) * LANES)
        for a in range(-1, KERNEL + 1):
            if 0 <= a < KERNEL:
                tap = (KERNEL - 1 - a) * KERNEL + KERNEL - 1 - b if backward else a * KERNEL + b
                block = jnp.where(eye, w_ref[tap : tap + 1, lanes], 0.0).astype(BF16)
            elif c < 2:
                block = empty
            else:
                continue
            for o in range(2):
                r = a + o
                if 0 <= r < 8:
                    at = (r // 2) * 1792 + b * 256 + (r % 2) * LANES
                    weights[c][at : at + LANES, o * LANES : (o + 1) * LANES] = block

    def product(c, q):
        return jnp.dot(
            lefts[c][32 * q : 32 * q + 512, :],
            weights[c][1792 * q : 1792 * (q + 1), :],
            preferred_element_type=F32,
        )

    def finish(c, acc):
        lanes = slice(c * LANES, (c + 1) * LANES)
        acc = acc.reshape(16, 32, 256)
        for slot in range(4):
            r, q = slot // 2, slot % 2
            for o in range(2):
                value = acc[8 * r : 8 * r + 8, 16 * q : 16 * q + 16, o * LANES : (o + 1) * LANES]
                if backward:
                    value = (value + last_ref[slot, :, o, :, lanes].astype(F32)) * (slot < count).astype(F32)
                else:
                    value = value + last_ref[:, lanes].reshape(1, 1, LANES)
                out_ref[slot, :, o, :, lanes] = value.astype(BF16)

    for c in range(blocks + 1):
        acc = None
        if c < blocks:
            fill(c)
        for q in range(4):
            if c:
                term = product(c - 1, q)
                acc = term if acc is None else acc + term
            if c < blocks:
                for b in range(2 * q, min(2 * q + 2, KERNEL)):
                    windows(c, b)
                    diagonals(c, b)
        if c < blocks and not backward:
            copies[c].start()
        if c:
            finish(c - 1, acc)
    if not backward:
        for copy in copies:
            copy.wait()


def taps_body(g_ref, left_ref, out_ref, paired, sums):
    for slot in range(4):
        r, q = slot // 2, slot % 2
        for o in range(2):
            paired[8 * r : 8 * r + 8, 16 * q : 16 * q + 16, o * LANES : (o + 1) * LANES] = g_ref[slot, :, o].astype(F32)
    turned = paired[...].reshape(512, 256).T.astype(BF16)
    group = lax.broadcasted_iota(jnp.int32, (8, LANES), 1) // 8
    place_in = lax.broadcasted_iota(jnp.int32, (8, LANES), 1) % 8 == lax.broadcasted_iota(jnp.int32, (8, LANES), 0)

    def product(q):
        return jnp.dot(turned, left_ref[0, 32 * q : 32 * q + 512, :], preferred_element_type=F32)

    def diagonals(q, prod):
        for b in range(KERNEL):
            for par in range(2):
                for o in range(2):
                    a = 2 * q + par - o
                    if not 0 <= a < KERNEL:
                        continue
                    cols = slice(b * 256 + par * LANES, b * 256 + (par + 1) * LANES)
                    value = prod[o * LANES : o * LANES + 8, cols]
                    for k in range(1, 16):
                        row = o * LANES + 8 * k
                        value = jnp.where(group == k, prod[row : row + 8, cols], value)
                    key = a * KERNEL + b
                    if o == 0:
                        sums[key] = value
                    else:
                        sums[key] = sums[key] + value

    ahead = product(0)
    for q in range(4):
        prod = ahead
        if q < 3:
            ahead = product(q + 1)
        diagonals(q, prod)
    total = jnp.sum(jnp.where(place_in[None], sums[...], 0.0), axis=1)
    out_ref[0:49, :] = total
    out_ref[49:64, :] = jnp.zeros((15, LANES), F32)


def pick(second, own, other):
    s = second.astype(F32)
    own = own.astype(F32)
    other = other.astype(F32)
    low = own * (1.0 - s) + other * s
    high = own * s + other * (1.0 - s)
    return jnp.concatenate([low, high], axis=1)


def store_turned(devices, out_ref, turned, cols):
    per = turned.shape[0] // devices
    if per % 16:
        out_ref[:, cols] = turned
        return
    odd = lax.axis_index("space") % 2
    half = turned.shape[0] // 2
    for d in range(devices):
        at = (d // 2) * per + jnp.where(odd == d % 2, 0, half)
        out_ref[pl.ds(pl.multiple_of(at, 16), per), cols] = turned[d * per : (d + 1) * per]


def grad_in_body(devices, own_ref, other_ref, w_ref, out_ref, turned_ref, full_ref):
    second = lax.axis_index("tensor") == 1
    for slot in range(4):
        rows = slice(slot * 256, slot * 256 + 256)
        full = pick(second, own_ref[rows, :], other_ref[rows, :]).astype(BF16)
        full_ref[rows, :] = full
        store_turned(devices, turned_ref, full.T, rows)
        out_ref[rows, :] = jnp.dot(full, w_ref[...], preferred_element_type=F32)


def grad_more_body(full_ref, w_ref, out_ref):
    out_ref[...] = jnp.dot(full_ref[...], w_ref[...], preferred_element_type=F32)


def in_lanes(columns, lanes):
    lane = lax.broadcasted_iota(jnp.int32, (columns[0].shape[0], lanes), 1)
    value = jnp.zeros(lane.shape, F32)
    for at, column in enumerate(columns):
        value = jnp.where(lane == at, column, value)
    return value


def norm_body(devices, own_ref, other_ref, gain_ref, shift_ref, out_ref, turned_ref, stats_ref):
    gain = gain_ref[...].reshape(1, -1)
    shift = shift_ref[...].reshape(1, -1)
    second = lax.axis_index("tensor") == 1
    for slot in range(4):
        rows = slice(slot * 256, slot * 256 + 256)
        full = pick(second, own_ref[rows, :], other_ref[rows, :])
        mean = jnp.mean(full, axis=1, keepdims=True)
        centered = full - mean
        var = jnp.mean(centered * centered, axis=1, keepdims=True)
        inverse = lax.rsqrt(var + 1e-06)
        stats_ref[rows, :] = in_lanes((mean, inverse), stats_ref.shape[1])
        value = (centered * inverse * gain + shift).astype(BF16)
        out_ref[rows, :] = value
        store_turned(devices, turned_ref, value.T, rows)


def chunk_body(normed_ref, up_ref, bias_ref, in_ref, grad_turned_ref, turned_ref, act_ref, pre_ref, keep_ref, send_ref):
    bias = bias_ref[...]
    half = keep_ref.shape[1]
    for slot in range(4):
        rows = slice(slot * 256, slot * 256 + 256)
        hidden = jnp.dot(normed_ref[rows, :], up_ref[...], preferred_element_type=F32) + bias
        phi, e = phi_pair(hidden)
        act_ref[rows, :] = (hidden * phi).astype(BF16)
        pre_ref[rows, :] = (in_ref[rows, :] * (phi + hidden * (e * DENSITY))).astype(BF16)
    for at, left, right in ((0, grad_turned_ref, act_ref), (1, turned_ref, pre_ref)):
        grad = jnp.dot(left[...], right[...], preferred_element_type=F32).astype(BF16)
        keep_ref[at] = grad[:half]
        send_ref[at] = grad[half:]


def split(second, value):
    half = value.shape[1] // 2
    s = second.astype(F32)
    low, high = value[:, :half], value[:, half:]
    return low * (1.0 - s) + high * s, low * s + high * (1.0 - s)


def turned_dot(values, w_ref):
    total = None
    for at, ref in enumerate(values):
        width = ref.shape[1]
        term = lax.dot_general(
            ref[...], w_ref[:, at * width : (at + 1) * width], (((1,), (1,)), ((), ())), preferred_element_type=F32
        )
        total = term if total is None else total + term
    return total


def back_body(own_ref, other_ref, stats_ref, gain_ref, up_ref, *rest):
    pres, (keep_ref, send_ref, more_ref, sums_ref) = rest[:CHUNKS], rest[CHUNKS:]
    second = lax.axis_index("tensor") == 1
    back = turned_dot(pres, up_ref)
    rows = pick(second, own_ref[...], other_ref[...])
    stats = stats_ref[...]
    normalized = (rows - stats[:, 0:1]) * stats[:, 1:2]
    scaled = back * gain_ref[...].reshape(1, -1)
    both = (jnp.sum(scaled, axis=1, keepdims=True), jnp.sum(scaled * normalized, axis=1, keepdims=True))
    sums_ref[...] = in_lanes(both, LANES)
    pieces = []
    for value in both:
        for _ in range(3):
            piece = value.astype(BF16).astype(F32)
            pieces.append(piece)
            value = value - piece
    half = keep_ref.shape[1]
    keep, send = split(second, back)
    keep_ref[...] = keep
    cut = send_ref.shape[1]
    send_ref[...] = send[:, :cut].astype(BF16)
    more_ref[:, : half - cut] = send[:, cut:].astype(BF16)
    more_ref[:, half - cut :] = in_lanes(pieces, LANES).astype(BF16)


def branch_body(down_ref, *rest):
    acts, (keep_ref, send_ref) = rest[:CHUNKS], rest[CHUNKS:]
    keep, send = split(lax.axis_index("tensor") == 1, turned_dot(acts, down_ref))
    keep_ref[...] = keep
    send_ref[...] = send.astype(BF16)


def first_body(keep_ref, got_ref, keep_out, send_out):
    bit = lax.axis_index("space") // 4
    for half in range(2):
        for out_ref, at in ((keep_out, 2 * bit + half), (send_out, 2 * (1 - bit) + half)):
            value = keep_ref[:, at].astype(F32) + got_ref[:, at].astype(F32)
            out_ref[:, half] = value.astype(out_ref.dtype)


def middle_body(keep_ref, got_ref, old_ref, old_got_ref, keep_out, send_out, old_out):
    bit = (lax.axis_index("space") // 2) % 2
    for half in range(2):
        for out_ref, at in ((keep_out, 2 * half + bit), (send_out, 2 * half + 1 - bit)):
            value = keep_ref[:, at].astype(F32) + got_ref[:, at].astype(F32)
            out_ref[:, half] = value.astype(out_ref.dtype)
    old_out[...] = old_ref[:, bit] + old_got_ref[:, bit].astype(F32)
    send_out[:, 2] = (old_ref[:, 1 - bit] + old_got_ref[:, 1 - bit].astype(F32)).astype(BF16)


def second_body(keep_ref, got_ref, old_ref, keep_out, send_out, old_out):
    bit = lax.axis_index("space") // 4
    keep_out[...] = keep_ref[:, bit] + got_ref[:, bit].astype(F32)
    send_out[...] = (keep_ref[:, 1 - bit] + got_ref[:, 1 - bit].astype(F32)).astype(BF16)
    old_out[...] = old_ref[...] + got_ref[:, 2].astype(F32)


def third_body(keep_ref, got_ref, out_ref):
    out_ref[...] = keep_ref[...] + got_ref[...].astype(F32)


def put_taps(value, send_ref, at):
    value = value.astype(BF16)
    rows = value.shape[0]
    for lanes in range(value.shape[1] // LANES):
        send_ref[at : at + rows, :] = value[:, lanes * LANES : (lanes + 1) * LANES]
        at += rows
    return value.astype(F32)


def got_taps(got_ref, at, shape):
    rows, width = shape
    parts = [got_ref[at + k * rows : at + (k + 1) * rows, :] for k in range(width // LANES)]
    return jnp.concatenate(parts, axis=1).astype(F32)


def first_taps_body(keep_ref, got_ref, taps_ref, taps_got_ref, keep_out, send_out, taps_out):
    bit = (lax.axis_index("space") // 2) % 2
    per, width = keep_ref.shape[2:]
    blocks = width // LANES
    for half in range(2):
        at = 2 * half + bit
        keep_out[:, half] = keep_ref[:, at].astype(F32) + got_ref[:, at].astype(F32)
        at = 2 * half + 1 - bit
        value = (keep_ref[:, at].astype(F32) + got_ref[:, at].astype(F32)).astype(BF16)
        for g in range(2):
            for lanes in range(blocks):
                row = ((g * 2 + half) * blocks + lanes) * per
                send_out[row : row + per, :] = value[g, :, lanes * LANES : (lanes + 1) * LANES]
    taps_out[...] = put_taps(taps_ref[...] + taps_got_ref[...], send_out, 4 * blocks * per)


def second_taps_body(keep_ref, got_ref, taps_ref, keep_out, send_out, taps_out):
    bit = lax.axis_index("space") // 4
    per, width = keep_ref.shape[2:]
    blocks = width // LANES
    for g in range(2):
        for lanes in range(blocks):
            cols = slice(lanes * LANES, (lanes + 1) * LANES)

            def got(half):
                row = pl.multiple_of(((g * 2 + half) * blocks + lanes) * per, 16)
                return got_ref[pl.ds(row, per), :].astype(F32)

            keep_out[g, :, cols] = keep_ref[g, bit, :, cols] + got(bit)
            row = (g * blocks + lanes) * per
            send_out[row : row + per, :] = (keep_ref[g, 1 - bit, :, cols] + got(1 - bit)).astype(BF16)
    total = taps_ref[...] + got_taps(got_ref, 4 * blocks * per, taps_ref.shape)
    taps_out[...] = put_taps(total, send_out, 2 * blocks * per)


def last_body(tissue_ref, *refs):
    *sums, keep_ref, got_ref, taps_ref, down_ref, up_ref, kernel_ref = refs
    tiles = tissue_ref[0]
    for at in range(1, tissue_ref.shape[0]):
        tiles = tiles + tissue_ref[at]
    scale = lax.rsqrt(jnp.full((8, LANES), 256.0, F32) * tiles.astype(F32))[0:1, 0:1]
    per, width = keep_ref.shape[1:]
    blocks = width // LANES
    for at, out_ref in enumerate((down_ref, up_ref)):
        for k, ref in enumerate(sums):
            out_ref[:, k * width : (k + 1) * width] = ref[at] * scale
        for lanes in range(blocks):
            cols = slice(lanes * LANES, (lanes + 1) * LANES)
            row = (at * blocks + lanes) * per
            value = keep_ref[at, :, cols] + got_ref[row : row + per, :].astype(F32)
            start = len(sums) * width + lanes * LANES
            out_ref[:, start : start + LANES] = value * scale
    total = taps_ref[...] + got_taps(got_ref, 2 * blocks * per, taps_ref.shape)
    kernel_ref[...] = (total * scale)[: kernel_ref.shape[0]]


def block_out_body(tissue_ref, x_ref, keep_ref, got_ref, scale_ref, bias_ref, out_ref):
    count = tissue_ref[lax.axis_index("space")]
    ok = (pl.program_id(0) < count).astype(F32)
    branch = keep_ref[...] + got_ref[...].astype(F32) + bias_ref[...].reshape(1, -1)
    value = (x_ref[...].astype(F32) + scale_ref[...].reshape(1, -1) * branch) * ok
    out_ref[...] = value.astype(BF16)


def norm_back_body(cols, tissue_ref, own_ref, stats_ref, keep_ref, got_ref, more_ref, sums_ref, gain_ref, out_ref, near_ref, far_ref):
    half = own_ref.shape[1]
    stats = stats_ref[...]
    inverse = stats[:, 1:2]
    normalized = (own_ref[...].astype(F32) - stats[:, 0:1]) * inverse
    got = jnp.concatenate([got_ref[...], more_ref[...]], axis=1).astype(F32)
    scaled = (keep_ref[...] + got[:, :half]) * gain_ref[...]
    sums = sums_ref[...]
    first = (sums[:, 0:1] + (got[:, half : half + 1] + got[:, half + 1 : half + 2] + got[:, half + 2 : half + 3])) / (2.0 * half)
    other = (sums[:, 1:2] + (got[:, half + 3 : half + 4] + got[:, half + 4 : half + 5] + got[:, half + 5 : half + 6])) / (2.0 * half)
    grad = inverse * (scaled - first - normalized * other)
    out_ref[...] = grad.astype(BF16)
    tile = grad.reshape(16, 16, grad.shape[1])
    odd_row, _, _ = place(cols, tissue_ref)
    slot = pl.program_id(0)
    for side in range(2):
        span = slice(side * 16, side * 16 + 16)

        @pl.when(slot == side)
        def _():
            top = tile[0:3].astype(BF16)

            @pl.when(odd_row == 0)
            def _():
                far_ref[:, span, :] = top

            @pl.when(odd_row == 1)
            def _():
                near_ref[:, span, :] = top

        @pl.when(slot == side + 2)
        def _():
            bottom = tile[13:16].astype(BF16)

            @pl.when(odd_row == 0)
            def _():
                near_ref[:, span, :] = bottom

            @pl.when(odd_row == 1)
            def _():
                far_ref[:, span, :] = bottom


def on_device(
    features, dw_kernel, dw_bias, ln_gain, ln_bias, w_up, up_bias, w_down, down_bias, layer_scale,
    cotangent, neighbors, tissue_count,
):
    tiles_dev, side, _, chans = features.shape
    units = w_up.shape[1]
    cells = tiles_dev * side * side
    devices = lax.axis_size("space")
    me = lax.axis_index("space")
    tensor_index = lax.axis_index("tensor")
    block_rows = max(d for d in range(1, math.isqrt(devices) + 1) if devices % d == 0)
    block_cols = devices // block_rows
    blocks = chans // LANES

    call = Chain()

    def sds(shape, dtype):
        return jax.ShapeDtypeStruct(shape, dtype)

    hbm = pltpu.HBM

    def pin(value):
        return pltpu.with_memory_space_constraint(value, pltpu.HBM)

    def across(value):
        return lax.ppermute(value, "tensor", [(0, 1), (1, 0)])

    def exchanged(value, bit):
        return lax.ppermute(value, "space", [(d, d ^ bit) for d in range(devices)])

    def paired(value, along_rows, round_at):
        size = block_rows if along_rows else block_cols
        pairs = []
        for d in range(devices):
            place = d // block_cols if along_rows else d % block_cols
            other = place + 1 if place % 2 == round_at else place - 1
            if 0 <= other < size:
                pairs.append((d, d + (other - place) * (block_cols if along_rows else 1)))
        if not pairs:
            return jnp.zeros_like(value)
        return lax.ppermute(value, "space", pairs)

    rim_shape = (RIM, 2 * side, chans)
    pack_shape = (160, chans)

    def sides(x, near, far, masked):
        return call(
            functools.partial(side_body, masked, block_cols),
            (1,),
            [smem(), whole(features.shape), whole(rim_shape), whole(rim_shape)],
            [whole(pack_shape)] * 2,
            [sds(pack_shape, BF16)] * 2,
            [pltpu.VMEM((40, 8, chans), F32), pltpu.VMEM((40, 8, chans), F32), pltpu.VMEM((20, 8, chans), F32)],
            (tissue, x, near, far),
        )

    split_shape = (4, 8, 2, side, chans)
    split_spec = pl.BlockSpec((4, 8, 2, side, LANES), lambda c: (0, 0, 0, 0, c))

    left_shape = (blocks, 608, 1792)

    def conv(x, near, far, one, two, last, backward):
        outs = [whole(split_shape)]
        shapes = [sds(split_shape, BF16)]
        scratch = [pltpu.VMEM((40, 48, LANES), F32)]
        if backward:
            scratch += [pltpu.VMEM((1,) + left_shape[1:], BF16)] * 2
        else:
            outs.append(pl.BlockSpec(memory_space=pltpu.HBM))
            scratch += [pltpu.VMEM(left_shape, BF16), pltpu.SemaphoreType.DMA((blocks,))]
            shapes.append(hbm(left_shape, BF16))
        scratch += [pltpu.VMEM((4 * 1792, 256), BF16)] * 2
        return call(
            functools.partial(conv_body, backward, block_cols),
            (1,),
            [
                smem(), whole(features.shape), whole(rim_shape), whole(rim_shape), whole(pack_shape), whole(pack_shape),
                whole((KERNEL * KERNEL, chans)), whole(last.shape),
            ],
            outs, shapes, scratch,
            (tissue, x, near, far, one, two, dw_kernel, last), CONV_BYTES, 100000000 if backward else 1000,
        )

    total = 2 * chans
    width = units // CHUNKS

    def at_chunk(shape, k):
        return pl.BlockSpec(shape, lambda *_: (0, k))

    tissue = pin(tissue_count)
    near_send, far_send, branch_grad = call(
        functools.partial(rims_body, block_cols),
        (1,),
        [smem(), whole(features.shape), whole((cells, chans)), whole((chans,))],
        [whole(rim_shape), whole(rim_shape), whole((cells, chans))],
        [sds(rim_shape, BF16), sds(rim_shape, BF16), sds((cells, chans), BF16)],
        [], (tissue, pin(features), pin(cotangent.reshape(cells, chans)), pin(layer_scale)),
    )
    near = paired(near_send, True, 0)
    far = paired(far_send, True, 1)
    other_grad = across(branch_grad)
    act_grads = [None] * CHUNKS
    act_grads[0], grad_turned, grad_full = call(
        functools.partial(grad_in_body, devices),
        (1,),
        [whole((cells, chans)), whole((cells, chans)), at_chunk((total, width), 0)],
        [whole((cells, width)), whole((total, cells)), whole((cells, total))],
        [sds((cells, width), F32), sds((total, cells), BF16), sds((cells, total), BF16)],
        [], (branch_grad, other_grad, pin(w_down)),
    )
    one_send, two_send = sides(features, near, far, True)
    one = paired(one_send, False, 0)
    two = paired(two_send, False, 1)

    def more(k):
        (act_grads[k],) = call(
            grad_more_body,
            (1,),
            [whole((cells, total)), at_chunk((total, width), k)],
            [whole((cells, width))],
            [sds((cells, width), F32)],
            [], (grad_full, w_down),
        )

    for k in range(1, CHUNKS - 1):
        more(k)
    conv_out, left = conv(features, near, far, one, two, dw_bias.reshape(1, chans), False)
    conv_own = conv_out.reshape(cells, chans)
    conv_other = across(conv_own)
    more(CHUNKS - 1)
    normed, normed_turned, stats = call(
        functools.partial(norm_body, devices),
        (1,),
        [whole((cells, chans)), whole((cells, chans)), whole((total,)), whole((total,))],
        [whole((cells, total)), whole((total, cells)), whole((cells, LANES))],
        [sds((cells, total), BF16), sds((total, cells), BF16), sds((cells, LANES), F32)],
        [], (conv_own, conv_other, ln_gain, ln_bias),
    )

    grad_scale = lax.rsqrt(F32(side * side) * jnp.sum(tissue_count).astype(F32))
    stepped = devices == 8
    per = total // devices
    acts, pres, kept, got = [], [], [], []
    for k in range(CHUNKS):
        act, pre, keep, send = call(
            chunk_body,
            (1,),
            [
                whole((cells, total)), at_chunk((total, width), k), at_chunk((1, width), k), whole((cells, width)),
                whole((total, cells)), whole((total, cells)),
            ],
            [whole((cells, width)), whole((cells, width)), whole((2, chans, width)), whole((2, chans, width))],
            [hbm((cells, width), BF16), sds((cells, width), BF16), sds((2, chans, width), BF16), hbm((2, chans, width), BF16)],
            [],
            (normed, w_up, up_bias.reshape(1, units), act_grads[k], grad_turned, normed_turned),
        )
        acts.append(act)
        pres.append(pre)
        kept.append(keep)
        got.append(exchanged(send, 1) if stepped else send)

    half_shape = (2, 2, per, width)
    row_shape = (2, per, width)

    def first(k):
        if stepped:
            shape = (2, 4, per, width)
            keep, send = call(
                first_body, (1,), [whole(shape)] * 2, [whole(half_shape)] * 2,
                [hbm(half_shape, F32), sds(half_shape, BF16)], [],
                (kept[k].reshape(shape), got[k].reshape(shape)),
            )
            kept[k], got[k] = keep, exchanged(send, 4)

    def middle(k):
        if stepped:
            shape = (2, 4, per, width)
            out = (2, 3, per, width)
            keep, send, kept[k - 1] = call(
                middle_body, (1,), [whole(shape)] * 2 + [whole(half_shape)] * 2,
                [whole(half_shape), whole(out), whole(row_shape)],
                [hbm(half_shape, F32), sds(out, BF16), hbm(row_shape, F32)], [],
                (kept[k].reshape(shape), got[k].reshape(shape), pin(kept[k - 1]), got[k - 1]),
            )
            kept[k], got[k] = keep, exchanged(send, 2)

    def second(k):
        if stepped:
            keep, send, kept[k - 1] = call(
                second_body, (1,), [whole(half_shape), whole((2, 3, per, width)), whole(row_shape)], [whole(row_shape)] * 3,
                [sds(row_shape, F32), sds(row_shape, BF16), sds(row_shape, F32)], [],
                (pin(kept[k]), got[k], pin(kept[k - 1])),
            )
            kept[k], got[k] = keep, exchanged(send, 4)

    def third(k):
        if stepped:
            out = (2, per, width)
            (kept[k],) = call(
                third_body, (1,), [whole(out)] * 2, [whole(out)], [sds(out, F32)], [], (kept[k], got[k])
            )

    def scattered(k):
        value = jnp.concatenate([kept[k], got[k]], axis=1)
        if devices & (devices - 1):
            return lax.psum_scatter(value.astype(F32), "space", scatter_dimension=1, tiled=True) * grad_scale
        value = value.reshape(2, devices, -1, width)
        bit = 1
        while bit < devices:
            halves = value.reshape(2, -1, 2, *value.shape[2:])
            high = (me // bit) % 2 == 1
            send = jnp.where(high, halves[:, :, 0], halves[:, :, 1])
            keep = jnp.where(high, halves[:, :, 1], halves[:, :, 0])
            value = keep.astype(F32) + exchanged(send, bit).astype(F32)
            bit *= 2
            if bit < devices:
                value = value.astype(BF16)
        return value.reshape(2, -1, width) * grad_scale

    row_block = pl.BlockSpec((256, chans), lambda i: (i, 0))
    sums_spec = pl.BlockSpec((256, LANES), lambda i: (i, 0))
    wide = (chans + LANES) // 2
    wide_block = pl.BlockSpec((256, wide), lambda i: (i, 0))
    chunk_rows = [pl.BlockSpec((256, width), lambda i: (i, 0))] * CHUNKS
    back_keep, back_send, back_more, sums = call(
        back_body,
        (tiles_dev,),
        [row_block, row_block, sums_spec, whole((total,)), whole((total, units))] + chunk_rows,
        [row_block, wide_block, wide_block, sums_spec],
        [hbm((cells, chans), F32), hbm((cells, wide), BF16), hbm((cells, wide), BF16), hbm((cells, LANES), F32)],
        [], (conv_own, conv_other, stats, ln_gain, w_up, *pres),
    )
    back_got = across(back_send), across(back_more)
    def first_taps(k):
        out = (2, 2, per, width)
        rows = 4 * per * width // LANES + taps.shape[0] * blocks
        shape = (2, 4, per, width)
        keep, send, value = call(
            first_taps_body, (1,), [whole(shape)] * 2 + [whole(taps.shape)] * 2,
            [whole(out), whole((rows, LANES)), whole(taps.shape)],
            [sds(out, F32), sds((rows, LANES), BF16), sds(taps.shape, F32)], [],
            (kept[k].reshape(shape), got[k].reshape(shape), taps, taps_got),
        )
        kept[k], got[k] = keep, exchanged(send, 2)
        return value

    def second_taps(k):
        out = (2, per, width)
        was = got[k].shape
        rows = 2 * per * width // LANES + taps.shape[0] * blocks
        keep, send, value = call(
            second_taps_body, (1,), [whole((2, 2, per, width)), whole(was), whole(taps.shape)],
            [whole(out), whole((rows, LANES)), whole(taps.shape)],
            [sds(out, F32), sds((rows, LANES), BF16), sds(taps.shape, F32)], [], (kept[k], got[k], taps),
        )
        kept[k], got[k] = keep, exchanged(send, 4)
        return value

    first(0)
    my_gain = lax.dynamic_slice_in_dim(ln_gain.reshape(1, total), lax.axis_index("tensor") * chans, chans, 1)
    conv_grad, near_send, far_send = call(
        functools.partial(norm_back_body, block_cols),
        (tiles_dev,),
        [smem(), row_block, sums_spec, row_block, wide_block, wide_block, sums_spec, whole((1, chans))],
        [row_block, whole(rim_shape), whole(rim_shape)],
        [sds((cells, chans), BF16), sds(rim_shape, BF16), sds(rim_shape, BF16)],
        [],
        (tissue, pin(conv_own), pin(stats), pin(back_keep), *back_got, pin(sums), my_gain),
    )
    near = paired(near_send, True, 0)
    far = paired(far_send, True, 1)
    (taps,) = call(
        taps_body,
        (blocks,),
        [split_spec, pl.BlockSpec((1, 608, 1792), lambda c: (c, 0, 0))],
        [pl.BlockSpec((64, LANES), lambda c: (0, c))],
        [sds((64, chans), F32)],
        [pltpu.VMEM((16, 32, 256), F32), pltpu.VMEM((KERNEL * KERNEL, 8, LANES), F32)],
        (conv_grad.reshape(split_shape), pin(left)),
    )
    taps_got = exchanged(taps, 1) if stepped else None
    conv_grad_tiles = conv_grad.reshape(features.shape)
    one_send, two_send = sides(conv_grad_tiles, near, far, False)
    one = paired(one_send, False, 0)
    two = paired(two_send, False, 1)
    middle(1)
    if stepped:
        taps = first_taps(2)
    second(1)
    branch_keep, branch_send = call(
        branch_body,
        (tiles_dev,),
        [whole((total, units))] + chunk_rows,
        [row_block, row_block],
        [sds((cells, chans), F32), sds((cells, chans), BF16)],
        [], (w_down, *acts),
    )
    branch_got = across(branch_send)
    if stepped:
        taps = second_taps(2)
    third(1)
    (grad_features,) = conv(
        conv_grad_tiles, near, far, one, two, cotangent.reshape(split_shape), True
    )
    grad_features = grad_features.reshape(features.shape)
    (block_out,) = call(
        block_out_body,
        (tiles_dev,),
        [smem(), row_block, row_block, row_block, whole((chans,)), whole((chans,))],
        [row_block],
        [sds((cells, chans), BF16)],
        [], (tissue, features.reshape(cells, chans), branch_keep, branch_got, layer_scale, down_bias),
    )
    block_out = block_out.reshape(features.shape)
    if stepped:
        kernel_shape = (KERNEL * KERNEL, chans)
        grad_down, grad_up, grad_kernel = call(
            last_body,
            (1,),
            [smem()] + [whole((2, per, width))] * CHUNKS + [whole(got[CHUNKS - 1].shape), whole(taps.shape)],
            [whole((per, units))] * 2 + [whole(kernel_shape)],
            [sds((per, units), F32)] * 2 + [sds(kernel_shape, F32)],
            [], (tissue, *kept, got[CHUNKS - 1], taps),
        )
    else:
        grad_kernel = lax.psum(taps, "space")[: KERNEL * KERNEL] * grad_scale
        grads = [scattered(k) for k in range(CHUNKS)]
        grad_down = jnp.concatenate([g[0] for g in grads], axis=1).reshape(-1, units)
        grad_up = jnp.concatenate([g[1] for g in grads], axis=1).reshape(-1, units)
    return (block_out, grad_features, grad_up, grad_down, grad_kernel)


def solution(mesh):
    return jax.shard_map(
        on_device,
        mesh=mesh,
        in_specs=(
            P(("slide", "space"), None, None, "tensor"),
            P(None, "tensor"),
            P("tensor"),
            P(),
            P(),
            P(None, "tensor"),
            P("tensor"),
            P(None, "tensor"),
            P("tensor"),
            P("tensor"),
            P(("slide", "space"), None, None, "tensor"),
            P("slide", None),
            P("slide"),
        ),
        out_specs=(
            P(("slide", "space"), None, None, "tensor"),
            P(("slide", "space"), None, None, "tensor"),
            P(("slide", "space"), "tensor"),
            P(("slide", "space"), "tensor"),
            P("slide", "tensor"),
        ),
        check_vma=False,
    )
```
